32 devices in a mesh: aa: 8 (over z, x), ba: 4 (over y, core).
Axes of the slice: x: 2, y: 2, z: 4, core: 2. Of those that a mesh axis runs over, the one named last changes fastest.
Arguments:
- snapshots: float32 [2048, 8192], P(('aa', 'ba')), may hold values from -125 to 125
Outputs:
- factors: float32 [8, 16, 16], replicated
- pod_modes: float32 [8, 16, 8192], P(None, None, ('aa', 'ba'))
The draws below stay inside these ranges and needn't reach their ends.
All inputs are finite; a program needn't handle non-finite values.
Results may differ from the reference program's by a relative error of at most 0.000098.
Values sent between devices are 32-bit elements; how exact they have to be, the bound alone decides.
A program may use at most 128 MiB of HBM per device.

```python
import math
import jax
import jax.numpy as jnp
from jax import lax

BLOCK = 256
FREQS = 8
BLOCKS = 8
TIMES = 2048
POINTS = 8192


def draw_snapshots(key, part):
    key_point = jax.random.fold_in(key, 11)
    key_block = jax.random.fold_in(key, 12)
    key_noise = jax.random.fold_in(key, 13)
    trend = 1.0 + 2.0 * jnp.arange(POINTS, dtype=jnp.float32) / POINTS
    point_scale = jnp.exp(jax.random.uniform(key_point, (POINTS,), jnp.float32, 0.0, math.log(10.0 / 3.0))) * trend
    block_scale = jnp.exp(jax.random.uniform(key_block, (TIMES // BLOCK,), jnp.float32, 0.0, math.log(10.0)))
    time_scale = jnp.repeat(block_scale, BLOCK)
    noise_field = jnp.clip(jax.random.normal(key_noise, (TIMES, POINTS), jnp.float32), -5.0, 5.0)
    return 0.25 * noise_field * time_scale[:, None] * point_scale[None, :]


def setup_inputs(seed: int = 0) -> dict:
    splits = jax.random.split(jax.random.key(seed), 2)
    return {
        "snapshots": draw_snapshots(jax.random.fold_in(splits[1], 71), 0),
    }


def spectral_table(block_len, points):
    sample = jnp.arange(block_len, dtype=jnp.int32)
    harmonic = jnp.arange(1, FREQS + 1, dtype=jnp.int32)
    phase_turns = (sample[:, None] * harmonic[None, :] % block_len).astype(jnp.float32) * (2.0 * math.pi / block_len)
    sample_angle = sample.astype(jnp.float32) * (2.0 * math.pi / block_len)
    window = 0.5 - 0.5 * jnp.cos(sample_angle)
    norm_scale = 1.0 / jnp.sqrt(points * jnp.sum(window * window))
    cosine = window[:, None] * jnp.cos(phase_turns) * norm_scale
    sine = -window[:, None] * jnp.sin(phase_turns) * norm_scale
    return jnp.stack([cosine, sine], axis=1)

def local_gram(spectra):
    columns = 2 * spectra.shape[0]
    product = jnp.einsum('bgfp,chfp->fbgch', spectra, spectra, precision=lax.Precision.HIGHEST)
    return product.reshape(FREQS, columns, columns)

def finish(spectra, gram_sum, points):
    blocks = spectra.shape[0]
    columns = 2 * blocks
    lower_factor = jnp.linalg.cholesky(gram_sum)
    identity = jnp.broadcast_to(jnp.eye(columns, dtype=gram_sum.dtype), lower_factor.shape)
    inverse = lax.linalg.triangular_solve(lower_factor, identity, left_side=True, lower=True)
    pod_modes = math.sqrt(points) * jnp.einsum('fibg,bgfp->fip', inverse.reshape(FREQS, columns, blocks, 2), spectra, precision=lax.Precision.HIGHEST)
    return (jnp.swapaxes(lower_factor, 1, 2), pod_modes)

def reference(snapshots):
    table = spectral_table(BLOCK, POINTS)
    arranged = snapshots.reshape(BLOCKS, BLOCK, POINTS)
    spectra = jnp.einsum('bsp,sgf->bgfp', arranged, table, precision=lax.Precision.HIGHEST)
    factors, pod_modes = finish(spectra, local_gram(spectra), POINTS)
    return (factors, pod_modes)
```

```python
import functools
import math

import jax
import jax.numpy as jnp
import ml_dtypes
import numpy as np
from jax import lax
from jax.experimental import pallas as pl
from jax.experimental.pallas import tpu as pltpu
from jax.sharding import PartitionSpec as P

FREQS = 8
MESH = pl.DeviceIdType.MESH
BF16 = jnp.bfloat16
F32 = jnp.float32

STEPS = ((2, 0), (2, 1), (1, 0), (1, 1), (3, 0), (3, 1), (0, 1), (0, 0))
LAG = 6


def spectral_table(block_len, points):
    sample = jnp.arange(block_len, dtype=jnp.int32)
    harmonic = jnp.arange(1, FREQS + 1, dtype=jnp.int32)
    phase_turns = (sample[:, None] * harmonic[None, :] % block_len).astype(jnp.float32) * (
        2.0 * math.pi / block_len
    )
    sample_angle = sample.astype(jnp.float32) * (2.0 * math.pi / block_len)
    window = 0.5 - 0.5 * jnp.cos(sample_angle)
    norm_scale = 1.0 / jnp.sqrt(points * jnp.sum(window * window))
    cosine = window[:, None] * jnp.cos(phase_turns) * norm_scale
    sine = -window[:, None] * jnp.sin(phase_turns) * norm_scale
    return jnp.stack([cosine, sine], axis=1)


def split_table(block_len, points, parts):
    sample = np.arange(block_len)
    harmonic = np.arange(1, FREQS + 1)
    turns = (harmonic[:, None] * sample[None, :] % block_len) * (2.0 * np.pi / block_len)
    window = 0.5 - 0.5 * np.cos(sample * (2.0 * np.pi / block_len))
    scale = window / np.sqrt(points * np.sum(window * window))
    full = np.stack([np.cos(turns) * scale, -np.sin(turns) * scale], axis=1)
    full = full.reshape(2 * FREQS, parts, block_len // parts).transpose(1, 0, 2).astype(np.float32)
    terms = []
    rest = full
    for _ in range(3):
        term = rest.astype(ml_dtypes.bfloat16)
        terms.append(term)
        rest = rest - term.astype(np.float32)
    rows = np.concatenate(terms, axis=1)
    return np.concatenate([rows] * 3, axis=2)


def split3(value):
    high = value.astype(BF16)
    rest = value - high.astype(F32)
    middle = rest.astype(BF16)
    low = (rest - middle.astype(F32)).astype(BF16)
    return high, middle, low


def kernel(
    points, x_hbm, table_hbm, factors_ref, modes_ref,
    x_buf, table, part, core_in, y_out, y_in, block_out, blocks,
    gram_out, gram_in, plane_out, plane_in, upper,
    in_sem, table_sem, core_send, core_recv, y_send, y_recv,
    block_send, block_recv, gram_send, gram_recv, plane_send, plane_recv,
):
    aa, ba = lax.axis_index("aa"), lax.axis_index("ba")
    z, x = aa // 2, aa % 2
    y, core = ba // 2, ba % 2
    other_core = 1 - core
    core_peer = (aa, y * 2 + other_core)
    y_peer = (aa, (1 - y) * 2 + core)
    owners = [((z + dz) % 4) * 2 + (x + dx) % 2 for dz, dx in STEPS]
    plane = [(i // 4, i // 2 % 2, i % 2) for i in range(8)]
    plane_ids = [
        (z * 2 + (x + dx) % 2, ((y + dy) % 2) * 2 + (core + dc) % 2) for dx, dy, dc in plane
    ]
    line_ids = [(((z + dz) % 4) * 2 + x, ba) for dz in range(4)]

    barrier = pltpu.get_barrier_semaphore()
    peers = [(owner, ba) for owner in owners[:-1]]
    peers += [plane_ids[i] for i in range(1, 8) if plane[i] != (1, 0, 0)]
    for peer in peers:
        pl.semaphore_signal(barrier, inc=1, device_id=peer, device_id_type=MESH)

    table_copy = pltpu.make_async_copy(table_hbm.at[ba], table, table_sem)
    table_copy.start()
    loads = []
    for tile in range(16):
        row, k = tile // 8, tile % 8
        side = (1 - y) if row == 0 else y
        start = pl.multiple_of(owners[k] * 1024 + side * 512, 512)
        load = pltpu.make_async_copy(x_hbm.at[:, pl.ds(start, 512)], x_buf.at[tile], in_sem.at[tile])
        load.start()
        loads.append(load)
    table_copy.wait()

    sends = []

    def remote(src, dst, send, recv, device):
        copy = pltpu.make_async_remote_copy(
            src_ref=src, dst_ref=dst, send_sem=send, recv_sem=recv,
            device_id=device, device_id_type=MESH,
        )
        copy.start()
        sends.append(copy)
        return copy

    core_copies = []
    y_copies = []

    def send_y(k):
        core_copies[k].wait_recv()
        y_out[k] = part[k, core] + core_in[k]
        y_copies.append(remote(y_out.at[k], y_in.at[k], y_send.at[k], y_recv.at[k], y_peer))

    for tile in range(16):
        loads[tile].wait()
        terms = jnp.concatenate(split3(x_buf[tile]), axis=0)
        rows = jnp.dot(table[...], terms, preferred_element_type=F32)
        total = rows[0:16] + rows[16:32] + rows[32:48]
        part[tile, 0] = total[:, 0:256]
        part[tile, 1] = total[:, 256:512]
        if tile == 0:
            pl.semaphore_wait(barrier, len(peers))
        core_copies.append(
            remote(
                part.at[tile, other_core], core_in.at[tile],
                core_send.at[tile], core_recv.at[tile], core_peer,
            )
        )
        if LAG <= tile < LAG + 8:
            send_y(tile - LAG)

    block_copies = []
    for k in range(8):
        core_copies[8 + k].wait_recv()
        y_copies[k].wait_recv()
        total = part[8 + k, core] + core_in[8 + k] + y_in[k]
        mine = pl.ds(pl.multiple_of(aa * 16, 16), 16)
        if k == 7:
            blocks[0, mine, :] = total[:, 0:128]
            blocks[1, mine, :] = total[:, 128:256]
        else:
            block_out[k, 0] = total[:, 0:128]
            block_out[k, 1] = total[:, 128:256]
            block_copies.append(
                remote(
                    block_out.at[k], blocks.at[:, mine, :],
                    block_send.at[k], block_recv.at[k], (owners[k], ba),
                )
            )
    for copy in block_copies:
        copy.wait_recv()

    columns = jnp.concatenate(
        [
            jnp.concatenate([blocks[half, pl.ds(r, 8, stride=16), :] for r in range(16)], axis=0)
            for half in range(2)
        ],
        axis=1,
    )
    high, middle, low = split3(columns)
    gram_full = lax.dot_general(
        jnp.concatenate([high, high, middle, middle, high, low], axis=1),
        jnp.concatenate([high, middle, high, middle, low, high], axis=1),
        (((1,), (1,)), ((), ())),
        preferred_element_type=F32,
    )
    row_freq = lax.broadcasted_iota(jnp.int32, (128, 128), 0) // 16
    lane_freq = lax.broadcasted_iota(jnp.int32, (128, 128), 1) // 16
    same = row_freq == lane_freq
    kept = jnp.where(same, gram_full, 0.0).reshape(8, 16, 128)
    gram_out[...] = ((kept[0] + kept[1]) + (kept[2] + kept[3])) + ((kept[4] + kept[5]) + (kept[6] + kept[7]))

    copies = [
        remote(gram_out, gram_in.at[i], gram_send.at[i], gram_recv.at[i], plane_ids[i]) for i in range(1, 8)
    ]
    for copy in copies:
        copy.wait_recv()
    pairs = [gram_out[...] + gram_in[1]] + [gram_in[i] + gram_in[i + 1] for i in (2, 4, 6)]
    plane_out[...] = (pairs[0] + pairs[1]) + (pairs[2] + pairs[3])
    copies = [
        remote(plane_out, plane_in.at[i], plane_send.at[i], plane_recv.at[i], line_ids[i]) for i in range(1, 4)
    ]
    for copy in copies:
        copy.wait_recv()
    gram = (plane_out[...] + plane_in[2]) + (plane_in[1] + plane_in[3])

    lane = lax.broadcasted_iota(jnp.int32, (16, 128), 1) % 16
    row = lax.broadcasted_iota(jnp.int32, (16, 128), 0)
    natural = (row % 8) * 2 + row // 8
    place = [(j % 2) * 8 + j // 2 for j in range(16)]
    left = [pltpu.roll(gram, (128 - place[j]) % 128, 1) if place[j] else gram for j in range(16)]
    right = [(row == place[j]).astype(F32) for j in range(16)]
    upper_all = jnp.zeros((16, 128), F32)
    inverse_all = jnp.zeros((16, 128), F32)
    for j in range(16):
        pivot = left[j][place[j]:place[j] + 1, :]
        root = lax.rsqrt(pivot)
        root = root * (1.5 - 0.5 * pivot * root * root)
        upper_row = left[j] * root
        inverse_row = right[j] * root
        for i in range(j + 1, 16):
            scale = upper_row[place[i]:place[i] + 1, :]
            left[i] = left[i] - scale * upper_row
            right[i] = right[i] - scale * inverse_row
        upper_row = jnp.where(natural >= j, upper_row, 0.0)
        if j:
            upper_row = pltpu.roll(upper_row, j, 1)
            inverse_row = pltpu.roll(inverse_row, j, 1)
        upper_all = jnp.where(lane == j, upper_row, upper_all)
        inverse_all = jnp.where(lane == j, inverse_row, inverse_all)

    upper[...] = jnp.zeros_like(upper)
    upper[pl.ds(0, 8, stride=2), :] = upper_all[0:8]
    upper[pl.ds(1, 8, stride=2), :] = upper_all[8:16]
    factors_ref[...] = jnp.transpose(upper[...])[:, 0:16].reshape(8, 16, 16)

    inverse_all = inverse_all * math.sqrt(points)
    wide = jnp.where(same, jnp.concatenate([inverse_all] * 8, axis=0), 0.0)
    w_high, w_middle, w_low = split3(jnp.transpose(wide))
    modes = lax.dot_general(
        jnp.concatenate([w_high, w_high, w_middle, w_middle, w_high, w_low], axis=1),
        jnp.concatenate([high, middle, high, middle, low, high], axis=0),
        (((1,), (0,)), ((), ())),
        preferred_element_type=F32,
    )
    modes_ref[...] = modes.reshape(8, 16, 256)
    for copy in sends:
        copy.wait_send()


def fused(snapshots):
    points = snapshots.shape[1]
    table = jnp.asarray(split_table(256, points, 4))
    dma = pltpu.SemaphoreType.DMA
    vmem = pltpu.VMEM
    return pl.pallas_call(
        functools.partial(kernel, points),
        out_shape=(
            jax.ShapeDtypeStruct((8, 16, 16), F32),
            jax.ShapeDtypeStruct((8, 16, 256), F32),
        ),
        in_specs=[pl.BlockSpec(memory_space=pl.ANY)] * 2,
        out_specs=(pl.BlockSpec(memory_space=pltpu.VMEM),) * 2,
        scratch_shapes=[
            vmem((16, 64, 512), F32),
            vmem((48, 192), BF16),
            vmem((16, 2, 16, 256), F32),
            vmem((16, 16, 256), F32),
            vmem((8, 16, 256), F32),
            vmem((8, 16, 256), F32),
            vmem((8, 2, 16, 128), F32),
            vmem((2, 128, 128), F32),
            vmem((16, 128), F32),
            vmem((8, 16, 128), F32),
            vmem((16, 128), F32),
            vmem((4, 16, 128), F32),
            vmem((128, 128), F32),
            dma((16,)),
            dma,
            dma((16,)),
            dma((16,)),
            dma((8,)),
            dma((8,)),
            dma((8,)),
            dma((8,)),
            dma((8,)),
            dma((8,)),
            dma((4,)),
            dma((4,)),
        ],
        compiler_params=pltpu.CompilerParams(
            collective_id=0, has_side_effects=True, vmem_limit_bytes=48 * 1024 * 1024
        ),
        name="welch_qr",
    )(snapshots, table)


def local(snapshots):
    time_dev, points = snapshots.shape
    n_aa = lax.axis_size("aa")
    n_ba = lax.axis_size("ba")
    if (n_aa, n_ba, time_dev, points) == (8, 4, 64, 8192):
        return fused(snapshots)
    pts_dev = points // (n_aa * n_ba)
    block_len = time_dev * n_ba
    table = spectral_table(block_len, points)
    regrouped = lax.all_to_all(
        lax.all_to_all(snapshots, "aa", split_axis=1, concat_axis=0, tiled=True),
        "ba",
        split_axis=1,
        concat_axis=0,
        tiled=True,
    )
    arranged = regrouped.reshape(n_ba, n_aa, time_dev, pts_dev)
    table_parts = table.reshape(n_ba, time_dev, 2, FREQS)
    spectra = jnp.einsum("uasp,usgf->agfp", arranged, table_parts, precision=lax.Precision.HIGHEST)
    blocks = spectra.shape[0]
    columns = 2 * blocks
    product = jnp.einsum("bgfp,chfp->fbgch", spectra, spectra, precision=lax.Precision.HIGHEST)
    gram_sum = lax.psum(product.reshape(FREQS, columns, columns), ("aa", "ba"))
    lower_factor = jnp.linalg.cholesky(gram_sum)
    identity = jnp.broadcast_to(jnp.eye(columns, dtype=gram_sum.dtype), lower_factor.shape)
    inverse = lax.linalg.triangular_solve(lower_factor, identity, left_side=True, lower=True)
    pod_modes = math.sqrt(points) * jnp.einsum(
        "fibg,bgfp->fip",
        inverse.reshape(FREQS, columns, blocks, 2),
        spectra,
        precision=lax.Precision.HIGHEST,
    )
    return (jnp.swapaxes(lower_factor, 1, 2), pod_modes)


def solution(mesh):
    placed = (P(("aa", "ba"), None),)
    return jax.shard_map(
        local,
        mesh=mesh,
        in_specs=placed,
        out_specs=(P(), P(None, None, ("aa", "ba"))),
        check_vma=False,
    )
```

```python
import functools
import math

import jax
import jax.numpy as jnp
import ml_dtypes
import numpy as np
from jax import lax
from jax.experimental import pallas as pl
from jax.experimental.pallas import tpu as pltpu
from jax.sharding import PartitionSpec as P

FREQS = 8
MESH = pl.DeviceIdType.MESH
BF16 = jnp.bfloat16
F32 = jnp.float32

STEPS = ((2, 0), (2, 1), (1, 0), (1, 1), (3, 0), (3, 1), (0, 1), (0, 0))
GROUPS = (
    ((0, 1), ()),
    ((2, 3), ()),
    ((4, 5, 6, 7), (0, 1, 2, 3)),
    ((8, 9, 10, 11), (4, 5, 6, 7)),
    ((12, 13, 14, 15), ()),
)


def spectral_table(block_len, points):
    sample = jnp.arange(block_len, dtype=jnp.int32)
    harmonic = jnp.arange(1, FREQS + 1, dtype=jnp.int32)
    phase_turns = (sample[:, None] * harmonic[None, :] % block_len).astype(jnp.float32) * (
        2.0 * math.pi / block_len
    )
    sample_angle = sample.astype(jnp.float32) * (2.0 * math.pi / block_len)
    window = 0.5 - 0.5 * jnp.cos(sample_angle)
    norm_scale = 1.0 / jnp.sqrt(points * jnp.sum(window * window))
    cosine = window[:, None] * jnp.cos(phase_turns) * norm_scale
    sine = -window[:, None] * jnp.sin(phase_turns) * norm_scale
    return jnp.stack([cosine, sine], axis=1)


def split_table(block_len, points, parts):
    sample = np.arange(block_len)
    harmonic = np.arange(1, FREQS + 1)
    turns = (harmonic[:, None] * sample[None, :] % block_len) * (2.0 * np.pi / block_len)
    window = 0.5 - 0.5 * np.cos(sample * (2.0 * np.pi / block_len))
    scale = window / np.sqrt(points * np.sum(window * window))
    full = np.stack([np.cos(turns) * scale, -np.sin(turns) * scale], axis=1)
    full = full.reshape(2 * FREQS, parts, block_len // parts).transpose(1, 0, 2).astype(np.float32)
    terms = []
    rest = full
    for _ in range(3):
        term = rest.astype(ml_dtypes.bfloat16)
        terms.append(term)
        rest = rest - term.astype(np.float32)
    rows = np.concatenate(terms, axis=1)
    return np.concatenate([rows] * 3, axis=2)


def split3(value):
    high = value.astype(BF16)
    rest = value - high.astype(F32)
    middle = rest.astype(BF16)
    low = (rest - middle.astype(F32)).astype(BF16)
    return high, middle, low


def kernel(
    points, x_hbm, table_hbm, factors_ref, modes_ref,
    x_buf, table, part, core_in, y_out, y_in, block_out, blocks,
    gram_out, gram_in, plane_out, plane_in, upper,
    in_sem, table_sem, core_send, core_recv, y_send, y_recv,
    block_send, block_recv, gram_send, gram_recv, plane_send, plane_recv,
):
    aa, ba = lax.axis_index("aa"), lax.axis_index("ba")
    z, x = aa // 2, aa % 2
    y, core = ba // 2, ba % 2
    other_core = 1 - core
    core_peer = (aa, y * 2 + other_core)
    y_peer = (aa, (1 - y) * 2 + core)
    owners = [((z + dz) % 4) * 2 + (x + dx) % 2 for dz, dx in STEPS]
    plane = [(i // 4, i // 2 % 2, i % 2) for i in range(8)]
    plane_ids = [
        (z * 2 + (x + dx) % 2, ((y + dy) % 2) * 2 + (core + dc) % 2) for dx, dy, dc in plane
    ]
    line_ids = [(((z + dz) % 4) * 2 + x, ba) for dz in range(4)]

    table_copy = pltpu.make_async_copy(table_hbm.at[ba], table, table_sem)
    table_copy.start()
    loads = []
    for tile in range(16):
        row, k = tile // 8, tile % 8
        side = (1 - y) if row == 0 else y
        start = pl.multiple_of(owners[k] * 1024 + side * 512, 512)
        load = pltpu.make_async_copy(x_hbm.at[:, pl.ds(start, 512)], x_buf.at[tile], in_sem.at[tile])
        load.start()
        loads.append(load)

    barrier = pltpu.get_barrier_semaphore()
    peers = [(owner, ba) for owner in owners[:-1]]
    peers += [plane_ids[i] for i in range(1, 8) if plane[i] != (1, 0, 0)]
    for peer in peers:
        pl.semaphore_signal(barrier, inc=1, device_id=peer, device_id_type=MESH)
    table_copy.wait()

    sends = []

    def remote(src, dst, send, recv, device):
        copy = pltpu.make_async_remote_copy(
            src_ref=src, dst_ref=dst, send_sem=send, recv_sem=recv,
            device_id=device, device_id_type=MESH,
        )
        copy.start()
        sends.append(copy)
        return copy

    core_copies = []
    y_copies = []

    def send_y(k):
        core_copies[k].wait_recv()
        y_out[k] = part[k, core] + core_in[k]
        y_copies.append(remote(y_out.at[k], y_in.at[k], y_send.at[k], y_recv.at[k], y_peer))

    for group, ready in GROUPS:
        for tile in group:
            loads[tile].wait()
        terms = [jnp.concatenate(split3(x_buf[tile]), axis=0) for tile in group]
        rows = jnp.dot(table[...], jnp.concatenate(terms, axis=1), preferred_element_type=F32)
        total = rows[0:16] + rows[16:32] + rows[32:48]
        for n, tile in enumerate(group):
            part[tile, 0] = total[:, n * 512:n * 512 + 256]
            part[tile, 1] = total[:, n * 512 + 256:n * 512 + 512]
        if group[0] == 0:
            pl.semaphore_wait(barrier, len(peers))
        for tile in group:
            core_copies.append(
                remote(
                    part.at[tile, other_core], core_in.at[tile],
                    core_send.at[tile], core_recv.at[tile], core_peer,
                )
            )
        for k in ready:
            send_y(k)

    block_copies = []
    for k in range(8):
        core_copies[8 + k].wait_recv()
        y_copies[k].wait_recv()
        total = part[8 + k, core] + core_in[8 + k] + y_in[k]
        mine = pl.ds(pl.multiple_of(aa * 16, 16), 16)
        if k == 7:
            blocks[0, mine, :] = total[:, 0:128]
            blocks[1, mine, :] = total[:, 128:256]
        else:
            block_out[k, 0] = total[:, 0:128]
            block_out[k, 1] = total[:, 128:256]
            block_copies.append(
                remote(
                    block_out.at[k], blocks.at[:, mine, :],
                    block_send.at[k], block_recv.at[k], (owners[k], ba),
                )
            )
    for copy in block_copies:
        copy.wait_recv()

    columns = jnp.concatenate(
        [
            jnp.concatenate([blocks[half, pl.ds(r, 8, stride=16), :] for r in range(16)], axis=0)
            for half in range(2)
        ],
        axis=1,
    )
    high, middle, low = split3(columns)
    contract_last = (((1,), (1,)), ((), ()))
    product = lax.dot_general(
        jnp.concatenate([high, middle, low], axis=0),
        jnp.concatenate([high, middle], axis=0),
        contract_last,
        preferred_element_type=F32,
    )
    high_low = lax.dot_general(high, low, contract_last, preferred_element_type=F32)
    gram_full = (product[0:128, 0:128] + product[128:256, 128:256]) + (
        (product[0:128, 128:256] + product[128:256, 0:128]) + (product[256:384, 0:128] + high_low)
    )
    row_freq = lax.broadcasted_iota(jnp.int32, (128, 128), 0) // 16
    lane_freq = lax.broadcasted_iota(jnp.int32, (128, 128), 1) // 16
    same = row_freq == lane_freq
    kept = jnp.where(same, gram_full, 0.0).reshape(8, 16, 128)
    gram_out[...] = ((kept[0] + kept[1]) + (kept[2] + kept[3])) + ((kept[4] + kept[5]) + (kept[6] + kept[7]))

    copies = [
        remote(gram_out, gram_in.at[i], gram_send.at[i], gram_recv.at[i], plane_ids[i]) for i in range(1, 8)
    ]
    for copy in copies:
        copy.wait_recv()
    pairs = [gram_out[...] + gram_in[1]] + [gram_in[i] + gram_in[i + 1] for i in (2, 4, 6)]
    plane_out[...] = (pairs[0] + pairs[1]) + (pairs[2] + pairs[3])
    copies = [
        remote(plane_out, plane_in.at[i], plane_send.at[i], plane_recv.at[i], line_ids[i]) for i in range(1, 4)
    ]
    for copy in copies:
        copy.wait_recv()
    gram = (plane_out[...] + plane_in[2]) + (plane_in[1] + plane_in[3])

    lane = lax.broadcasted_iota(jnp.int32, (16, 128), 1) % 16
    row = lax.broadcasted_iota(jnp.int32, (16, 128), 0)
    natural = (row % 8) * 2 + row // 8
    place = [(j % 2) * 8 + j // 2 for j in range(16)]
    left = [pltpu.roll(gram, (128 - place[j]) % 128, 1) if place[j] else gram for j in range(16)]
    right = [(row == place[j]).astype(F32) for j in range(16)]
    upper_all = jnp.zeros((16, 128), F32)
    inverse_all = jnp.zeros((16, 128), F32)
    for j in range(16):
        pivot = left[j][place[j]:place[j] + 1, :]
        root = lax.rsqrt(pivot)
        root = root * (1.5 - 0.5 * pivot * root * root)
        upper_row = left[j] * root
        inverse_row = right[j] * root
        for i in range(j + 1, 16):
            scale = upper_row[place[i]:place[i] + 1, :]
            left[i] = left[i] - scale * upper_row
            right[i] = right[i] - scale * inverse_row
        upper_row = jnp.where(natural >= j, upper_row, 0.0)
        if j:
            upper_row = pltpu.roll(upper_row, j, 1)
            inverse_row = pltpu.roll(inverse_row, j, 1)
        upper_all = jnp.where(lane == j, upper_row, upper_all)
        inverse_all = jnp.where(lane == j, inverse_row, inverse_all)

    upper[...] = jnp.zeros_like(upper)
    upper[pl.ds(0, 8, stride=2), :] = upper_all[0:8]
    upper[pl.ds(1, 8, stride=2), :] = upper_all[8:16]
    factors_ref[...] = jnp.transpose(upper[...])[:, 0:16].reshape(8, 16, 16)

    inverse_all = inverse_all * math.sqrt(points)
    wide = jnp.where(same, jnp.concatenate([inverse_all] * 8, axis=0), 0.0)
    w_high, w_middle, w_low = split3(jnp.transpose(wide))
    modes = lax.dot_general(
        jnp.concatenate([w_high, w_high, w_middle, w_middle, w_high, w_low], axis=1),
        jnp.concatenate([high, middle, high, middle, low, high], axis=0),
        (((1,), (0,)), ((), ())),
        preferred_element_type=F32,
    )
    modes_ref[...] = modes.reshape(8, 16, 256)
    for copy in sends:
        copy.wait_send()


def fused(snapshots):
    points = snapshots.shape[1]
    table = jnp.asarray(split_table(256, points, 4))
    dma = pltpu.SemaphoreType.DMA
    vmem = pltpu.VMEM
    return pl.pallas_call(
        functools.partial(kernel, points),
        out_shape=(
            jax.ShapeDtypeStruct((8, 16, 16), F32),
            jax.ShapeDtypeStruct((8, 16, 256), F32),
        ),
        in_specs=[pl.BlockSpec(memory_space=pltpu.HBM)] * 2,
        out_specs=(pl.BlockSpec(memory_space=pltpu.VMEM),) * 2,
        scratch_shapes=[
            vmem((16, 64, 512), F32),
            vmem((48, 192), BF16),
            vmem((16, 2, 16, 256), F32),
            vmem((16, 16, 256), F32),
            vmem((8, 16, 256), F32),
            vmem((8, 16, 256), F32),
            vmem((8, 2, 16, 128), F32),
            vmem((2, 128, 128), F32),
            vmem((16, 128), F32),
            vmem((8, 16, 128), F32),
            vmem((16, 128), F32),
            vmem((4, 16, 128), F32),
            vmem((128, 128), F32),
            dma((16,)),
            dma,
            dma((16,)),
            dma((16,)),
            dma((8,)),
            dma((8,)),
            dma((8,)),
            dma((8,)),
            dma((8,)),
            dma((8,)),
            dma((4,)),
            dma((4,)),
        ],
        compiler_params=pltpu.CompilerParams(
            collective_id=0, has_side_effects=True, vmem_limit_bytes=48 * 1024 * 1024
        ),
        name="welch_qr",
    )(snapshots, table)


def local(snapshots):
    time_dev, points = snapshots.shape
    n_aa = lax.axis_size("aa")
    n_ba = lax.axis_size("ba")
    if (n_aa, n_ba, time_dev, points) == (8, 4, 64, 8192):
        return fused(snapshots)
    pts_dev = points // (n_aa * n_ba)
    block_len = time_dev * n_ba
    table = spectral_table(block_len, points)
    regrouped = lax.all_to_all(
        lax.all_to_all(snapshots, "aa", split_axis=1, concat_axis=0, tiled=True),
        "ba",
        split_axis=1,
        concat_axis=0,
        tiled=True,
    )
    arranged = regrouped.reshape(n_ba, n_aa, time_dev, pts_dev)
    table_parts = table.reshape(n_ba, time_dev, 2, FREQS)
    spectra = jnp.einsum("uasp,usgf->agfp", arranged, table_parts, precision=lax.Precision.HIGHEST)
    blocks = spectra.shape[0]
    columns = 2 * blocks
    product = jnp.einsum("bgfp,chfp->fbgch", spectra, spectra, precision=lax.Precision.HIGHEST)
    gram_sum = lax.psum(product.reshape(FREQS, columns, columns), ("aa", "ba"))
    lower_factor = jnp.linalg.cholesky(gram_sum)
    identity = jnp.broadcast_to(jnp.eye(columns, dtype=gram_sum.dtype), lower_factor.shape)
    inverse = lax.linalg.triangular_solve(lower_factor, identity, left_side=True, lower=True)
    pod_modes = math.sqrt(points) * jnp.einsum(
        "fibg,bgfp->fip",
        inverse.reshape(FREQS, columns, blocks, 2),
        spectra,
        precision=lax.Precision.HIGHEST,
    )
    return (jnp.swapaxes(lower_factor, 1, 2), pod_modes)


def solution(mesh):
    placed = (P(("aa", "ba"), None),)
    return jax.shard_map(
        local,
        mesh=mesh,
        in_specs=placed,
        out_specs=(P(), P(None, None, ("aa", "ba"))),
        check_vma=False,
    )
```

```python
import functools
import math

import jax
import jax.numpy as jnp
from jax import lax
from jax.experimental import pallas as pl
from jax.experimental.pallas import tpu as pltpu
from jax.sharding import PartitionSpec as P

FREQS = 8
MESH = pl.DeviceIdType.MESH
BF16 = jnp.bfloat16
F32 = jnp.float32

STEPS = ((2, 0), (2, 1), (1, 0), (1, 1), (3, 0), (3, 1), (0, 1), (0, 0))
GROUPS = (
    ((0, 1), ()),
    ((2, 3), ()),
    ((4, 5, 6, 7), (0, 1, 2, 3)),
    ((8, 9, 10, 11), (4, 5, 6, 7)),
    ((12, 13, 14, 15), ()),
)


def spectral_table(block_len, points):
    sample = jnp.arange(block_len, dtype=jnp.int32)
    harmonic = jnp.arange(1, FREQS + 1, dtype=jnp.int32)
    phase_turns = (sample[:, None] * harmonic[None, :] % block_len).astype(jnp.float32) * (
        2.0 * math.pi / block_len
    )
    sample_angle = sample.astype(jnp.float32) * (2.0 * math.pi / block_len)
    window = 0.5 - 0.5 * jnp.cos(sample_angle)
    norm_scale = 1.0 / jnp.sqrt(points * jnp.sum(window * window))
    cosine = window[:, None] * jnp.cos(phase_turns) * norm_scale
    sine = -window[:, None] * jnp.sin(phase_turns) * norm_scale
    return jnp.stack([cosine, sine], axis=1)


def split_table(ba, points):
    row = lax.broadcasted_iota(jnp.int32, (16, 64), 0)
    sample = lax.broadcasted_iota(jnp.int32, (16, 64), 1) + ba * 64
    turns = (sample * (row // 2 + 1) + 64 * (row % 2)) % 256
    step = 2.0 * math.pi / 256
    window = 0.5 - 0.5 * jnp.cos(sample.astype(F32) * step)
    power = sum((0.5 - 0.5 * math.cos(n * step)) ** 2 for n in range(256))
    value = window * jnp.cos(turns.astype(F32) * step) * (1.0 / math.sqrt(points * power))
    rows = jnp.concatenate(split3(value), axis=0)
    return jnp.concatenate([rows] * 3, axis=1)


def split3(value):
    high = value.astype(BF16)
    rest = value - high.astype(F32)
    middle = rest.astype(BF16)
    low = (rest - middle.astype(F32)).astype(BF16)
    return high, middle, low


def kernel(
    points, x_hbm, factors_ref, modes_ref,
    x_buf, table, part, core_in, y_out, y_in, block_out, blocks,
    gram_out, gram_in, plane_out, plane_in, upper,
    in_sem, core_send, core_recv, y_send, y_recv,
    block_send, block_recv, gram_send, gram_recv, plane_send, plane_recv,
):
    aa, ba = lax.axis_index("aa"), lax.axis_index("ba")
    z, x = aa // 2, aa % 2
    y, core = ba // 2, ba % 2
    other_core = 1 - core
    core_peer = (aa, y * 2 + other_core)
    y_peer = (aa, (1 - y) * 2 + core)
    owners = [((z + dz) % 4) * 2 + (x + dx) % 2 for dz, dx in STEPS]
    plane = [(i // 4, i // 2 % 2, i % 2) for i in range(8)]
    plane_ids = [
        (z * 2 + (x + dx) % 2, ((y + dy) % 2) * 2 + (core + dc) % 2) for dx, dy, dc in plane
    ]
    line_ids = [(((z + dz) % 4) * 2 + x, ba) for dz in range(4)]

    loads = []
    for tile in range(16):
        row, k = tile // 8, tile % 8
        side = (1 - y) if row == 0 else y
        start = pl.multiple_of(owners[k] * 1024 + side * 512, 512)
        load = pltpu.make_async_copy(x_hbm.at[:, pl.ds(start, 512)], x_buf.at[tile], in_sem.at[tile])
        load.start()
        loads.append(load)

    barrier = pltpu.get_barrier_semaphore()
    peers = [(owner, ba) for owner in owners[:-1]]
    peers += [plane_ids[i] for i in range(1, 8) if plane[i] != (1, 0, 0)]
    for peer in peers:
        pl.semaphore_signal(barrier, inc=1, device_id=peer, device_id_type=MESH)
    table[...] = split_table(ba, points)

    sends = []

    def remote(src, dst, send, recv, device):
        copy = pltpu.make_async_remote_copy(
            src_ref=src, dst_ref=dst, send_sem=send, recv_sem=recv,
            device_id=device, device_id_type=MESH,
        )
        copy.start()
        sends.append(copy)
        return copy

    core_copies = []
    y_copies = []

    def send_y(k):
        core_copies[k].wait_recv()
        y_out[k] = part[k, core] + core_in[k]
        y_copies.append(remote(y_out.at[k], y_in.at[k], y_send.at[k], y_recv.at[k], y_peer))

    for group, ready in GROUPS:
        for tile in group:
            loads[tile].wait()
        terms = [jnp.concatenate(split3(x_buf[tile]), axis=0) for tile in group]
        rows = jnp.dot(table[...], jnp.concatenate(terms, axis=1), preferred_element_type=F32)
        total = rows[0:16] + rows[16:32] + rows[32:48]
        for n, tile in enumerate(group):
            part[tile, 0] = total[:, n * 512:n * 512 + 256]
            part[tile, 1] = total[:, n * 512 + 256:n * 512 + 512]
        if group[0] == 0:
            pl.semaphore_wait(barrier, len(peers))
        for tile in group:
            core_copies.append(
                remote(
                    part.at[tile, other_core], core_in.at[tile],
                    core_send.at[tile], core_recv.at[tile], core_peer,
                )
            )
        for k in ready:
            send_y(k)

    block_copies = []
    for k in range(8):
        core_copies[8 + k].wait_recv()
        y_copies[k].wait_recv()
        total = part[8 + k, core] + core_in[8 + k] + y_in[k]
        mine = pl.ds(pl.multiple_of(aa * 16, 16), 16)
        if k == 7:
            blocks[0, mine, :] = total[:, 0:128]
            blocks[1, mine, :] = total[:, 128:256]
        else:
            block_out[k, 0] = total[:, 0:128]
            block_out[k, 1] = total[:, 128:256]
            block_copies.append(
                remote(
                    block_out.at[k], blocks.at[:, mine, :],
                    block_send.at[k], block_recv.at[k], (owners[k], ba),
                )
            )
    for copy in block_copies:
        copy.wait_recv()

    columns = jnp.concatenate(
        [
            jnp.concatenate([blocks[half, pl.ds(r, 8, stride=16), :] for r in range(16)], axis=0)
            for half in range(2)
        ],
        axis=1,
    )
    high, middle, low = split3(columns)
    contract_last = (((1,), (1,)), ((), ()))
    product = lax.dot_general(
        jnp.concatenate([high, middle, low], axis=0),
        jnp.concatenate([high, middle], axis=0),
        contract_last,
        preferred_element_type=F32,
    )
    high_low = lax.dot_general(high, low, contract_last, preferred_element_type=F32)
    gram_full = (product[0:128, 0:128] + product[128:256, 128:256]) + (
        (product[0:128, 128:256] + product[128:256, 0:128]) + (product[256:384, 0:128] + high_low)
    )
    row_freq = lax.broadcasted_iota(jnp.int32, (128, 128), 0) // 16
    lane_freq = lax.broadcasted_iota(jnp.int32, (128, 128), 1) // 16
    same = row_freq == lane_freq
    kept = jnp.where(same, gram_full, 0.0).reshape(8, 16, 128)
    gram_out[...] = ((kept[0] + kept[1]) + (kept[2] + kept[3])) + ((kept[4] + kept[5]) + (kept[6] + kept[7]))

    copies = [
        remote(gram_out, gram_in.at[i], gram_send.at[i], gram_recv.at[i], plane_ids[i]) for i in range(1, 8)
    ]
    for copy in copies:
        copy.wait_recv()
    pairs = [gram_out[...] + gram_in[1]] + [gram_in[i] + gram_in[i + 1] for i in (2, 4, 6)]
    plane_out[...] = (pairs[0] + pairs[1]) + (pairs[2] + pairs[3])
    copies = [
        remote(plane_out, plane_in.at[i], plane_send.at[i], plane_recv.at[i], line_ids[i]) for i in range(1, 4)
    ]
    for copy in copies:
        copy.wait_recv()
    gram = (plane_out[...] + plane_in[2]) + (plane_in[1] + plane_in[3])

    lane = lax.broadcasted_iota(jnp.int32, (16, 128), 1) % 16
    row = lax.broadcasted_iota(jnp.int32, (16, 128), 0)
    natural = (row % 8) * 2 + row // 8
    place = [(j % 2) * 8 + j // 2 for j in range(16)]
    left = [pltpu.roll(gram, (128 - place[j]) % 128, 1) if place[j] else gram for j in range(16)]
    right = [(row == place[j]).astype(F32) for j in range(16)]
    upper_all = jnp.zeros((16, 128), F32)
    inverse_all = jnp.zeros((16, 128), F32)
    for j in range(16):
        pivot = left[j][place[j]:place[j] + 1, :]
        root = lax.rsqrt(pivot)
        root = root * (1.5 - 0.5 * pivot * root * root)
        upper_row = left[j] * root
        inverse_row = right[j] * root
        for i in range(j + 1, 16):
            scale = upper_row[place[i]:place[i] + 1, :]
            left[i] = left[i] - scale * upper_row
            right[i] = right[i] - scale * inverse_row
        upper_row = jnp.where(natural >= j, upper_row, 0.0)
        if j:
            upper_row = pltpu.roll(upper_row, j, 1)
            inverse_row = pltpu.roll(inverse_row, j, 1)
        upper_all = jnp.where(lane == j, upper_row, upper_all)
        inverse_all = jnp.where(lane == j, inverse_row, inverse_all)

    upper[...] = jnp.zeros_like(upper)
    upper[pl.ds(0, 8, stride=2), :] = upper_all[0:8]
    upper[pl.ds(1, 8, stride=2), :] = upper_all[8:16]
    factors_ref[...] = jnp.transpose(upper[...])[:, 0:16].reshape(8, 16, 16)

    inverse_all = inverse_all * math.sqrt(points)
    wide = jnp.where(same, jnp.concatenate([inverse_all] * 8, axis=0), 0.0)
    w_high, w_middle, w_low = split3(jnp.transpose(wide))
    modes = lax.dot_general(
        jnp.concatenate([w_high, w_high, w_middle, w_middle, w_high, w_low], axis=1),
        jnp.concatenate([high, middle, high, middle, low, high], axis=0),
        (((1,), (0,)), ((), ())),
        preferred_element_type=F32,
    )
    modes_ref[...] = modes.reshape(8, 16, 256)
    for copy in sends:
        copy.wait_send()


def fused(snapshots):
    points = snapshots.shape[1]
    dma = pltpu.SemaphoreType.DMA
    vmem = pltpu.VMEM
    return pl.pallas_call(
        functools.partial(kernel, points),
        out_shape=(
            jax.ShapeDtypeStruct((8, 16, 16), F32),
            jax.ShapeDtypeStruct((8, 16, 256), F32),
        ),
        in_specs=[pl.BlockSpec(memory_space=pltpu.HBM)],
        out_specs=(pl.BlockSpec(memory_space=pltpu.VMEM),) * 2,
        scratch_shapes=[
            vmem((16, 64, 512), F32),
            vmem((48, 192), BF16),
            vmem((16, 2, 16, 256), F32),
            vmem((16, 16, 256), F32),
            vmem((8, 16, 256), F32),
            vmem((8, 16, 256), F32),
            vmem((8, 2, 16, 128), F32),
            vmem((2, 128, 128), F32),
            vmem((16, 128), F32),
            vmem((8, 16, 128), F32),
            vmem((16, 128), F32),
            vmem((4, 16, 128), F32),
            vmem((128, 128), F32),
            dma((16,)),
            dma((16,)),
            dma((16,)),
            dma((8,)),
            dma((8,)),
            dma((8,)),
            dma((8,)),
            dma((8,)),
            dma((8,)),
            dma((4,)),
            dma((4,)),
        ],
        compiler_params=pltpu.CompilerParams(
            collective_id=0, has_side_effects=True, vmem_limit_bytes=63 * 1024 * 1024
        ),
        name="welch_qr",
    )(snapshots)


def local(snapshots):
    time_dev, points = snapshots.shape
    n_aa = lax.axis_size("aa")
    n_ba = lax.axis_size("ba")
    if (n_aa, n_ba, time_dev, points) == (8, 4, 64, 8192):
        return fused(snapshots)
    pts_dev = points // (n_aa * n_ba)
    block_len = time_dev * n_ba
    table = spectral_table(block_len, points)
    regrouped = lax.all_to_all(
        lax.all_to_all(snapshots, "aa", split_axis=1, concat_axis=0, tiled=True),
        "ba",
        split_axis=1,
        concat_axis=0,
        tiled=True,
    )
    arranged = regrouped.reshape(n_ba, n_aa, time_dev, pts_dev)
    table_parts = table.reshape(n_ba, time_dev, 2, FREQS)
    spectra = jnp.einsum("uasp,usgf->agfp", arranged, table_parts, precision=lax.Precision.HIGHEST)
    blocks = spectra.shape[0]
    columns = 2 * blocks
    product = jnp.einsum("bgfp,chfp->fbgch", spectra, spectra, precision=lax.Precision.HIGHEST)
    gram_sum = lax.psum(product.reshape(FREQS, columns, columns), ("aa", "ba"))
    lower_factor = jnp.linalg.cholesky(gram_sum)
    identity = jnp.broadcast_to(jnp.eye(columns, dtype=gram_sum.dtype), lower_factor.shape)
    inverse = lax.linalg.triangular_solve(lower_factor, identity, left_side=True, lower=True)
    pod_modes = math.sqrt(points) * jnp.einsum(
        "fibg,bgfp->fip",
        inverse.reshape(FREQS, columns, blocks, 2),
        spectra,
        precision=lax.Precision.HIGHEST,
    )
    return (jnp.swapaxes(lower_factor, 1, 2), pod_modes)


def solution(mesh):
    placed = (P(("aa", "ba"), None),)
    return jax.shard_map(
        local,
        mesh=mesh,
        in_specs=placed,
        out_specs=(P(), P(None, None, ("aa", "ba"))),
        check_vma=False,
    )
```

```python
import functools
import math

import jax
import jax.numpy as jnp
from jax import lax
from jax.experimental import pallas as pl
from jax.experimental.pallas import tpu as pltpu
from jax.sharding import PartitionSpec as P

FREQS = 8
MESH = pl.DeviceIdType.MESH
BF16 = jnp.bfloat16
F32 = jnp.float32

STEPS = ((2, 0), (2, 1), (1, 0), (1, 1), (3, 0), (3, 1), (0, 1), (0, 0))
GROUPS = (
    ((0, 1), ()),
    ((2, 3), ()),
    ((4, 5, 6, 7), (0, 1, 2, 3)),
    ((8, 9, 10, 11), (4, 5, 6, 7)),
    ((12, 13, 14, 15), ()),
)


def spectral_table(block_len, points):
    sample = jnp.arange(block_len, dtype=jnp.int32)
    harmonic = jnp.arange(1, FREQS + 1, dtype=jnp.int32)
    phase_turns = (sample[:, None] * harmonic[None, :] % block_len).astype(jnp.float32) * (
        2.0 * math.pi / block_len
    )
    sample_angle = sample.astype(jnp.float32) * (2.0 * math.pi / block_len)
    window = 0.5 - 0.5 * jnp.cos(sample_angle)
    norm_scale = 1.0 / jnp.sqrt(points * jnp.sum(window * window))
    cosine = window[:, None] * jnp.cos(phase_turns) * norm_scale
    sine = -window[:, None] * jnp.sin(phase_turns) * norm_scale
    return jnp.stack([cosine, sine], axis=1)


def split_table(ba, points):
    row = lax.broadcasted_iota(jnp.int32, (16, 64), 0)
    sample = lax.broadcasted_iota(jnp.int32, (16, 64), 1) + ba * 64
    turns = (sample * (row // 2 + 1) + 64 * (row % 2)) % 256
    step = 2.0 * math.pi / 256
    window = 0.5 - 0.5 * jnp.cos(sample.astype(F32) * step)
    power = sum((0.5 - 0.5 * math.cos(n * step)) ** 2 for n in range(256))
    value = window * jnp.cos(turns.astype(F32) * step) * (1.0 / math.sqrt(points * power))
    rows = jnp.concatenate(split3(value), axis=0)
    return jnp.concatenate([rows] * 3, axis=1)


def split3(value):
    high = value.astype(BF16)
    rest = value - high.astype(F32)
    middle = rest.astype(BF16)
    low = (rest - middle.astype(F32)).astype(BF16)
    return high, middle, low


def kernel(
    points, x_hbm, columns_hbm, gram_ref,
    x_buf, table, part, core_in, y_out, y_in, block_out, blocks,
    columns_buf, gram_out, gram_in, plane_out, plane_in,
    in_sem, columns_sem, core_send, core_recv, y_send, y_recv,
    block_send, block_recv, gram_send, gram_recv, plane_send, plane_recv,
):
    aa, ba = lax.axis_index("aa"), lax.axis_index("ba")
    z, x = aa // 2, aa % 2
    y, core = ba // 2, ba % 2
    other_core = 1 - core
    core_peer = (aa, y * 2 + other_core)
    y_peer = (aa, (1 - y) * 2 + core)
    owners = [((z + dz) % 4) * 2 + (x + dx) % 2 for dz, dx in STEPS]
    plane = [(i // 4, i // 2 % 2, i % 2) for i in range(8)]
    plane_ids = [
        (z * 2 + (x + dx) % 2, ((y + dy) % 2) * 2 + (core + dc) % 2) for dx, dy, dc in plane
    ]
    line_ids = [(((z + dz) % 4) * 2 + x, ba) for dz in range(4)]

    loads = []
    for tile in range(16):
        row, k = tile // 8, tile % 8
        side = (1 - y) if row == 0 else y
        start = pl.multiple_of(owners[k] * 1024 + side * 512, 512)
        load = pltpu.make_async_copy(x_hbm.at[:, pl.ds(start, 512)], x_buf.at[tile], in_sem.at[tile])
        load.start()
        loads.append(load)

    barrier = pltpu.get_barrier_semaphore()
    peers = [(owner, ba) for owner in owners[:-1]]
    peers += [plane_ids[i] for i in range(1, 8) if plane[i] != (1, 0, 0)]
    for peer in peers:
        pl.semaphore_signal(barrier, inc=1, device_id=peer, device_id_type=MESH)
    table[...] = split_table(ba, points)

    sends = []

    def remote(src, dst, send, recv, device):
        copy = pltpu.make_async_remote_copy(
            src_ref=src, dst_ref=dst, send_sem=send, recv_sem=recv,
            device_id=device, device_id_type=MESH,
        )
        copy.start()
        sends.append(copy)
        return copy

    core_copies = []
    y_copies = []

    def send_y(k):
        core_copies[k].wait_recv()
        y_out[k] = part[k, core] + core_in[k]
        y_copies.append(remote(y_out.at[k], y_in.at[k], y_send.at[k], y_recv.at[k], y_peer))

    for group, ready in GROUPS:
        for tile in group:
            loads[tile].wait()
        terms = [jnp.concatenate(split3(x_buf[tile]), axis=0) for tile in group]
        rows = jnp.dot(table[...], jnp.concatenate(terms, axis=1), preferred_element_type=F32)
        total = rows[0:16] + rows[16:32] + rows[32:48]
        for n, tile in enumerate(group):
            part[tile, 0] = total[:, n * 512:n * 512 + 256]
            part[tile, 1] = total[:, n * 512 + 256:n * 512 + 512]
        if group[0] == 0:
            pl.semaphore_wait(barrier, len(peers))
        for tile in group:
            core_copies.append(
                remote(
                    part.at[tile, other_core], core_in.at[tile],
                    core_send.at[tile], core_recv.at[tile], core_peer,
                )
            )
        for k in ready:
            send_y(k)

    block_copies = []
    for k in range(8):
        core_copies[8 + k].wait_recv()
        y_copies[k].wait_recv()
        total = part[8 + k, core] + core_in[8 + k] + y_in[k]
        mine = pl.ds(pl.multiple_of(aa * 16, 16), 16)
        if k == 7:
            blocks[0, mine, :] = total[:, 0:128]
            blocks[1, mine, :] = total[:, 128:256]
        else:
            block_out[k, 0] = total[:, 0:128]
            block_out[k, 1] = total[:, 128:256]
            block_copies.append(
                remote(
                    block_out.at[k], blocks.at[:, mine, :],
                    block_send.at[k], block_recv.at[k], (owners[k], ba),
                )
            )
    for copy in block_copies:
        copy.wait_recv()

    columns = jnp.concatenate(
        [
            jnp.concatenate([blocks[half, pl.ds(r, 8, stride=16), :] for r in range(16)], axis=0)
            for half in range(2)
        ],
        axis=1,
    )
    columns_buf[...] = columns
    columns_copy = pltpu.make_async_copy(columns_buf, columns_hbm, columns_sem)
    columns_copy.start()
    high, middle, low = split3(columns)
    contract_last = (((1,), (1,)), ((), ()))
    product = lax.dot_general(
        jnp.concatenate([high, middle, low], axis=0),
        jnp.concatenate([high, middle], axis=0),
        contract_last,
        preferred_element_type=F32,
    )
    high_low = lax.dot_general(high, low, contract_last, preferred_element_type=F32)
    gram_full = (product[0:128, 0:128] + product[128:256, 128:256]) + (
        (product[0:128, 128:256] + product[128:256, 0:128]) + (product[256:384, 0:128] + high_low)
    )
    row_freq = lax.broadcasted_iota(jnp.int32, (128, 128), 0) // 16
    lane_freq = lax.broadcasted_iota(jnp.int32, (128, 128), 1) // 16
    same = row_freq == lane_freq
    kept = jnp.where(same, gram_full, 0.0).reshape(8, 16, 128)
    gram_out[...] = ((kept[0] + kept[1]) + (kept[2] + kept[3])) + ((kept[4] + kept[5]) + (kept[6] + kept[7]))

    copies = [
        remote(gram_out, gram_in.at[i], gram_send.at[i], gram_recv.at[i], plane_ids[i]) for i in range(1, 8)
    ]
    for copy in copies:
        copy.wait_recv()
    pairs = [gram_out[...] + gram_in[1]] + [gram_in[i] + gram_in[i + 1] for i in (2, 4, 6)]
    plane_out[...] = (pairs[0] + pairs[1]) + (pairs[2] + pairs[3])
    copies = [
        remote(plane_out, plane_in.at[i], plane_send.at[i], plane_recv.at[i], line_ids[i]) for i in range(1, 4)
    ]
    for copy in copies:
        copy.wait_recv()
    gram_ref[...] = (plane_out[...] + plane_in[2]) + (plane_in[1] + plane_in[3])
    columns_copy.wait()
    for copy in sends:
        copy.wait_send()


def finish_kernel(points, gram_ref, columns_hbm, factors_hbm, modes_hbm, columns, upper, factors, modes, sems):
    load = pltpu.make_async_copy(columns_hbm, columns, sems.at[0])
    load.start()
    gram = gram_ref[...]
    lane = lax.broadcasted_iota(jnp.int32, (16, 128), 1) % 16
    row = lax.broadcasted_iota(jnp.int32, (16, 128), 0)
    natural = (row % 8) * 2 + row // 8
    place = [(j % 2) * 8 + j // 2 for j in range(16)]
    left = [pltpu.roll(gram, (128 - place[j]) % 128, 1) if place[j] else gram for j in range(16)]
    right = [(row == place[j]).astype(F32) for j in range(16)]
    upper_all = jnp.zeros((16, 128), F32)
    inverse_all = jnp.zeros((16, 128), F32)
    for j in range(16):
        pivot = left[j][place[j]:place[j] + 1, :]
        root = lax.rsqrt(pivot)
        root = root * (1.5 - 0.5 * pivot * root * root)
        upper_row = left[j] * root
        inverse_row = right[j] * root
        for i in range(j + 1, 16):
            scale = upper_row[place[i]:place[i] + 1, :]
            left[i] = left[i] - scale * upper_row
            right[i] = right[i] - scale * inverse_row
        upper_row = jnp.where(natural >= j, upper_row, 0.0)
        if j:
            upper_row = pltpu.roll(upper_row, j, 1)
            inverse_row = pltpu.roll(inverse_row, j, 1)
        upper_all = jnp.where(lane == j, upper_row, upper_all)
        inverse_all = jnp.where(lane == j, inverse_row, inverse_all)

    upper[...] = jnp.zeros_like(upper)
    upper[pl.ds(0, 8, stride=2), :] = upper_all[0:8]
    upper[pl.ds(1, 8, stride=2), :] = upper_all[8:16]
    factors[...] = jnp.transpose(upper[...])[:, 0:16].reshape(8, 16, 16)
    factors_copy = pltpu.make_async_copy(factors, factors_hbm, sems.at[1])
    factors_copy.start()

    inverse_all = inverse_all * math.sqrt(points)
    row_freq = lax.broadcasted_iota(jnp.int32, (128, 128), 0) // 16
    lane_freq = lax.broadcasted_iota(jnp.int32, (128, 128), 1) // 16
    wide = jnp.where(row_freq == lane_freq, jnp.concatenate([inverse_all] * 8, axis=0), 0.0)
    w_high, w_middle, w_low = split3(jnp.transpose(wide))
    load.wait()
    high, middle, low = split3(columns[...])
    product = lax.dot_general(
        jnp.concatenate([w_high, w_high, w_middle, w_middle, w_high, w_low], axis=1),
        jnp.concatenate([high, middle, high, middle, low, high], axis=0),
        (((1,), (0,)), ((), ())),
        preferred_element_type=F32,
    )
    modes[...] = product.reshape(8, 16, 256)
    modes_copy = pltpu.make_async_copy(modes, modes_hbm, sems.at[2])
    modes_copy.start()
    factors_copy.wait()
    modes_copy.wait()


def fused(snapshots):
    points = snapshots.shape[1]
    dma = pltpu.SemaphoreType.DMA
    vmem = pltpu.VMEM
    columns, gram = pl.pallas_call(
        functools.partial(kernel, points),
        out_shape=(
            jax.ShapeDtypeStruct((128, 256), F32),
            jax.ShapeDtypeStruct((16, 128), F32),
        ),
        in_specs=[pl.BlockSpec(memory_space=pltpu.HBM)],
        out_specs=(pl.BlockSpec(memory_space=pl.ANY), pl.BlockSpec(memory_space=pltpu.VMEM)),
        scratch_shapes=[
            vmem((16, 64, 512), F32),
            vmem((48, 192), BF16),
            vmem((16, 2, 16, 256), F32),
            vmem((16, 16, 256), F32),
            vmem((8, 16, 256), F32),
            vmem((8, 16, 256), F32),
            vmem((8, 2, 16, 128), F32),
            vmem((2, 128, 128), F32),
            vmem((128, 256), F32),
            vmem((16, 128), F32),
            vmem((8, 16, 128), F32),
            vmem((16, 128), F32),
            vmem((4, 16, 128), F32),
            dma((16,)),
            dma,
            dma((16,)),
            dma((16,)),
            dma((8,)),
            dma((8,)),
            dma((8,)),
            dma((8,)),
            dma((8,)),
            dma((8,)),
            dma((4,)),
            dma((4,)),
        ],
        compiler_params=pltpu.CompilerParams(
            collective_id=0, has_side_effects=True, vmem_limit_bytes=53 * 1024 * 1024
        ),
        name="welch_gram",
    )(snapshots)
    return pl.pallas_call(
        functools.partial(finish_kernel, points),
        out_shape=(
            jax.ShapeDtypeStruct((8, 16, 16), F32),
            jax.ShapeDtypeStruct((8, 16, 256), F32),
        ),
        in_specs=[pl.BlockSpec(memory_space=pltpu.VMEM), pl.BlockSpec(memory_space=pl.ANY)],
        out_specs=(pl.BlockSpec(memory_space=pl.ANY),) * 2,
        scratch_shapes=[
            vmem((128, 256), F32),
            vmem((128, 128), F32),
            vmem((8, 16, 16), F32),
            vmem((8, 16, 256), F32),
            dma((3,)),
        ],
        compiler_params=pltpu.CompilerParams(vmem_limit_bytes=16 * 1024 * 1024),
        name="factor_modes",
    )(gram, columns)


def local(snapshots):
    time_dev, points = snapshots.shape
    n_aa = lax.axis_size("aa")
    n_ba = lax.axis_size("ba")
    if (n_aa, n_ba, time_dev, points) == (8, 4, 64, 8192):
        return fused(snapshots)
    pts_dev = points // (n_aa * n_ba)
    block_len = time_dev * n_ba
    table = spectral_table(block_len, points)
    regrouped = lax.all_to_all(
        lax.all_to_all(snapshots, "aa", split_axis=1, concat_axis=0, tiled=True),
        "ba",
        split_axis=1,
        concat_axis=0,
        tiled=True,
    )
    arranged = regrouped.reshape(n_ba, n_aa, time_dev, pts_dev)
    table_parts = table.reshape(n_ba, time_dev, 2, FREQS)
    spectra = jnp.einsum("uasp,usgf->agfp", arranged, table_parts, precision=lax.Precision.HIGHEST)
    blocks = spectra.shape[0]
    columns = 2 * blocks
    product = jnp.einsum("bgfp,chfp->fbgch", spectra, spectra, precision=lax.Precision.HIGHEST)
    gram_sum = lax.psum(product.reshape(FREQS, columns, columns), ("aa", "ba"))
    lower_factor = jnp.linalg.cholesky(gram_sum)
    identity = jnp.broadcast_to(jnp.eye(columns, dtype=gram_sum.dtype), lower_factor.shape)
    inverse = lax.linalg.triangular_solve(lower_factor, identity, left_side=True, lower=True)
    pod_modes = math.sqrt(points) * jnp.einsum(
        "fibg,bgfp->fip",
        inverse.reshape(FREQS, columns, blocks, 2),
        spectra,
        precision=lax.Precision.HIGHEST,
    )
    return (jnp.swapaxes(lower_factor, 1, 2), pod_modes)


def solution(mesh):
    placed = (P(("aa", "ba"), None),)
    return jax.shard_map(
        local,
        mesh=mesh,
        in_specs=placed,
        out_specs=(P(), P(None, None, ("aa", "ba"))),
        check_vma=False,
    )
```

```python
import functools
import math

import jax
import jax.numpy as jnp
from jax import lax
from jax.experimental import pallas as pl
from jax.experimental.pallas import tpu as pltpu
from jax.sharding import PartitionSpec as P

FREQS = 8
MESH = pl.DeviceIdType.MESH
BF16 = jnp.bfloat16
F32 = jnp.float32

STEPS = ((2, 0), (2, 1), (1, 0), (1, 1), (3, 0), (3, 1), (0, 1), (0, 0))
GROUPS = (
    ((0,), ()),
    ((1,), ()),
    ((2, 3), (0,)),
    ((4, 5), (1, 2)),
    ((6, 7), (3, 4, 5, 6, 7)),
)


def spectral_table(block_len, points):
    sample = jnp.arange(block_len, dtype=jnp.int32)
    harmonic = jnp.arange(1, FREQS + 1, dtype=jnp.int32)
    phase_turns = (sample[:, None] * harmonic[None, :] % block_len).astype(jnp.float32) * (
        2.0 * math.pi / block_len
    )
    sample_angle = sample.astype(jnp.float32) * (2.0 * math.pi / block_len)
    window = 0.5 - 0.5 * jnp.cos(sample_angle)
    norm_scale = 1.0 / jnp.sqrt(points * jnp.sum(window * window))
    cosine = window[:, None] * jnp.cos(phase_turns) * norm_scale
    sine = -window[:, None] * jnp.sin(phase_turns) * norm_scale
    return jnp.stack([cosine, sine], axis=1)


def split_table(ba, points):
    row = lax.broadcasted_iota(jnp.int32, (16, 64), 0)
    sample = lax.broadcasted_iota(jnp.int32, (16, 64), 1) + ba * 64
    turns = (sample * (row // 2 + 1) + 64 * (row % 2)) % 256
    step = 2.0 * math.pi / 256
    window = 0.5 - 0.5 * jnp.cos(sample.astype(F32) * step)
    power = sum((0.5 - 0.5 * math.cos(n * step)) ** 2 for n in range(256))
    value = window * jnp.cos(turns.astype(F32) * step) * (1.0 / math.sqrt(points * power))
    rows = jnp.concatenate(split3(value), axis=0)
    return jnp.concatenate([rows] * 3, axis=1)


def split3(value):
    high = value.astype(BF16)
    rest = value - high.astype(F32)
    middle = rest.astype(BF16)
    low = (rest - middle.astype(F32)).astype(BF16)
    return high, middle, low


def kernel(
    points, x_hbm, columns_hbm, gram_ref,
    x_buf, table, part, core_in, y_out, y_in, block_out, blocks,
    columns_buf, gram_out, gram_in, plane_out, plane_in,
    in_sem, columns_sem, core_send, core_recv, y_send, y_recv,
    block_send, block_recv, gram_send, gram_recv, plane_send, plane_recv,
):
    aa, ba = lax.axis_index("aa"), lax.axis_index("ba")
    z, x = aa // 2, aa % 2
    y, core = ba // 2, ba % 2
    other_core = 1 - core
    core_peer = (aa, y * 2 + other_core)
    y_peer = (aa, (1 - y) * 2 + core)
    owners = [((z + dz) % 4) * 2 + (x + dx) % 2 for dz, dx in STEPS]
    plane = [(i // 4, i // 2 % 2, i % 2) for i in range(8)]
    plane_ids = [
        (z * 2 + (x + dx) % 2, ((y + dy) % 2) * 2 + (core + dc) % 2) for dx, dy, dc in plane
    ]
    line_ids = [(((z + dz) % 4) * 2 + x, ba) for dz in range(4)]

    barrier = pltpu.get_barrier_semaphore()
    peers = [(owner, ba) for owner in owners[:-1]]
    peers += [plane_ids[i] for i in range(1, 8) if plane[i] != (1, 0, 0)]
    for peer in peers:
        pl.semaphore_signal(barrier, inc=1, device_id=peer, device_id_type=MESH)
    loads = []
    for k in range(8):
        start = pl.multiple_of(owners[k] * 1024, 1024)
        load = pltpu.make_async_copy(x_hbm.at[:, pl.ds(start, 1024)], x_buf.at[k], in_sem.at[k])
        load.start()
        loads.append(load)
    table[...] = split_table(ba, points)

    sends = []

    def remote(src, dst, send, recv, device):
        copy = pltpu.make_async_remote_copy(
            src_ref=src, dst_ref=dst, send_sem=send, recv_sem=recv,
            device_id=device, device_id_type=MESH,
        )
        copy.start()
        sends.append(copy)
        return copy

    core_copies = []
    y_copies = []

    def send_y(k):
        core_copies[k].wait_recv()
        y_out[k] = part[k, core, 1 - y] + core_in[k, 1 - y]
        y_copies.append(remote(y_out.at[k], y_in.at[k], y_send.at[k], y_recv.at[k], y_peer))

    for group, ready in GROUPS:
        for tile in group:
            loads[tile].wait()
        terms = [jnp.concatenate(split3(x_buf[tile]), axis=0) for tile in group]
        rows = jnp.dot(table[...], jnp.concatenate(terms, axis=1), preferred_element_type=F32)
        total = rows[0:16] + rows[16:32] + rows[32:48]
        for n, tile in enumerate(group):
            for half in range(4):
                at = n * 1024 + half * 256
                part[tile, half % 2, half // 2] = total[:, at:at + 256]
        if group[0] == 0:
            pl.semaphore_wait(barrier, len(peers))
        for tile in group:
            core_copies.append(
                remote(
                    part.at[tile, other_core], core_in.at[tile],
                    core_send.at[tile], core_recv.at[tile], core_peer,
                )
            )
        for k in ready:
            send_y(k)

    block_copies = []
    for k in range(8):
        y_copies[k].wait_recv()
        total = part[k, core, y] + core_in[k, y] + y_in[k]
        mine = pl.ds(pl.multiple_of(aa * 16, 16), 16)
        if k == 7:
            blocks[0, mine, :] = total[:, 0:128]
            blocks[1, mine, :] = total[:, 128:256]
        else:
            block_out[k, 0] = total[:, 0:128]
            block_out[k, 1] = total[:, 128:256]
            block_copies.append(
                remote(
                    block_out.at[k], blocks.at[:, mine, :],
                    block_send.at[k], block_recv.at[k], (owners[k], ba),
                )
            )
    for copy in block_copies:
        copy.wait_recv()

    columns = jnp.concatenate(
        [
            jnp.concatenate([blocks[half, pl.ds(r, 8, stride=16), :] for r in range(16)], axis=0)
            for half in range(2)
        ],
        axis=1,
    )
    columns_buf[...] = columns
    columns_copy = pltpu.make_async_copy(columns_buf, columns_hbm, columns_sem)
    columns_copy.start()
    high, middle, low = split3(columns)
    contract_last = (((1,), (1,)), ((), ()))
    product = lax.dot_general(
        jnp.concatenate([high, middle, low], axis=0),
        jnp.concatenate([high, middle], axis=0),
        contract_last,
        preferred_element_type=F32,
    )
    high_low = lax.dot_general(high, low, contract_last, preferred_element_type=F32)
    gram_full = (product[0:128, 0:128] + product[128:256, 128:256]) + (
        (product[0:128, 128:256] + product[128:256, 0:128]) + (product[256:384, 0:128] + high_low)
    )
    row_freq = lax.broadcasted_iota(jnp.int32, (128, 128), 0) // 16
    lane_freq = lax.broadcasted_iota(jnp.int32, (128, 128), 1) // 16
    same = row_freq == lane_freq
    kept = jnp.where(same, gram_full, 0.0).reshape(8, 16, 128)
    gram_out[...] = ((kept[0] + kept[1]) + (kept[2] + kept[3])) + ((kept[4] + kept[5]) + (kept[6] + kept[7]))

    copies = [
        remote(gram_out, gram_in.at[i], gram_send.at[i], gram_recv.at[i], plane_ids[i]) for i in range(1, 8)
    ]
    for copy in sends[:-7]:
        copy.wait_send()
    for copy in copies:
        copy.wait_recv()
    pairs = [gram_out[...] + gram_in[1]] + [gram_in[i] + gram_in[i + 1] for i in (2, 4, 6)]
    plane_out[...] = (pairs[0] + pairs[1]) + (pairs[2] + pairs[3])
    copies = [
        remote(plane_out, plane_in.at[i], plane_send.at[i], plane_recv.at[i], line_ids[i]) for i in range(1, 4)
    ]
    columns_copy.wait()
    for copy in sends[-10:-3]:
        copy.wait_send()
    for copy in copies:
        copy.wait_recv()
    gram_ref[...] = (plane_out[...] + plane_in[2]) + (plane_in[1] + plane_in[3])
    for copy in sends[-3:]:
        copy.wait_send()


def finish_kernel(points, gram_ref, columns_hbm, factors_hbm, modes_hbm, columns, upper, factors, modes, sems):
    load = pltpu.make_async_copy(columns_hbm, columns, sems.at[0])
    load.start()
    gram = gram_ref[...]
    lane = lax.broadcasted_iota(jnp.int32, (16, 128), 1) % 16
    row = lax.broadcasted_iota(jnp.int32, (16, 128), 0)
    natural = (row % 8) * 2 + row // 8
    place = [(j % 2) * 8 + j // 2 for j in range(16)]
    left = [pltpu.roll(gram, (128 - place[j]) % 128, 1) if place[j] else gram for j in range(16)]
    right = [(row == place[j]).astype(F32) for j in range(16)]
    upper_all = jnp.zeros((16, 128), F32)
    inverse_all = jnp.zeros((16, 128), F32)
    for j in range(16):
        pivot = left[j][place[j]:place[j] + 1, :]
        root = lax.rsqrt(pivot)
        root = root * (1.5 - 0.5 * pivot * root * root)
        upper_row = left[j] * root
        inverse_row = right[j] * root
        for i in range(j + 1, 16):
            scale = upper_row[place[i]:place[i] + 1, :]
            left[i] = left[i] - scale * upper_row
            right[i] = right[i] - scale * inverse_row
        upper_row = jnp.where(natural >= j, upper_row, 0.0)
        if j:
            upper_row = pltpu.roll(upper_row, j, 1)
            inverse_row = pltpu.roll(inverse_row, j, 1)
        upper_all = jnp.where(lane == j, upper_row, upper_all)
        inverse_all = jnp.where(lane == j, inverse_row, inverse_all)

    upper[...] = jnp.zeros_like(upper)
    upper[pl.ds(0, 8, stride=2), :] = upper_all[0:8]
    upper[pl.ds(1, 8, stride=2), :] = upper_all[8:16]
    factors[...] = jnp.transpose(upper[...])[:, 0:16].reshape(8, 16, 16)
    factors_copy = pltpu.make_async_copy(factors, factors_hbm, sems.at[1])
    factors_copy.start()

    inverse_all = inverse_all * math.sqrt(points)
    row_freq = lax.broadcasted_iota(jnp.int32, (128, 128), 0) // 16
    lane_freq = lax.broadcasted_iota(jnp.int32, (128, 128), 1) // 16
    wide = jnp.where(row_freq == lane_freq, jnp.concatenate([inverse_all] * 8, axis=0), 0.0)
    w_high, w_middle, w_low = split3(jnp.transpose(wide))
    load.wait()
    high, middle, low = split3(columns[...])
    product = lax.dot_general(
        jnp.concatenate([w_high, w_high, w_middle, w_middle, w_high, w_low], axis=1),
        jnp.concatenate([high, middle, high, middle, low, high], axis=0),
        (((1,), (0,)), ((), ())),
        preferred_element_type=F32,
    )
    modes[...] = product.reshape(8, 16, 256)
    modes_copy = pltpu.make_async_copy(modes, modes_hbm, sems.at[2])
    modes_copy.start()
    factors_copy.wait()
    modes_copy.wait()


def fused(snapshots):
    points = snapshots.shape[1]
    dma = pltpu.SemaphoreType.DMA
    vmem = pltpu.VMEM
    columns, gram = pl.pallas_call(
        functools.partial(kernel, points),
        out_shape=(
            jax.ShapeDtypeStruct((128, 256), F32),
            jax.ShapeDtypeStruct((16, 128), F32),
        ),
        in_specs=[pl.BlockSpec(memory_space=pltpu.HBM)],
        out_specs=(pl.BlockSpec(memory_space=pl.ANY), pl.BlockSpec(memory_space=pltpu.VMEM)),
        scratch_shapes=[
            vmem((8, 64, 1024), F32),
            vmem((48, 192), BF16),
            vmem((8, 2, 2, 16, 256), F32),
            vmem((8, 2, 16, 256), F32),
            vmem((8, 16, 256), F32),
            vmem((8, 16, 256), F32),
            vmem((8, 2, 16, 128), F32),
            vmem((2, 128, 128), F32),
            vmem((128, 256), F32),
            vmem((16, 128), F32),
            vmem((8, 16, 128), F32),
            vmem((16, 128), F32),
            vmem((4, 16, 128), F32),
            dma((8,)),
            dma,
            dma((8,)),
            dma((8,)),
            dma((8,)),
            dma((8,)),
            dma((8,)),
            dma((8,)),
            dma((8,)),
            dma((8,)),
            dma((4,)),
            dma((4,)),
        ],
        compiler_params=pltpu.CompilerParams(
            collective_id=0, has_side_effects=True, vmem_limit_bytes=53 * 1024 * 1024
        ),
        name="welch_gram",
    )(snapshots)
    return pl.pallas_call(
        functools.partial(finish_kernel, points),
        out_shape=(
            jax.ShapeDtypeStruct((8, 16, 16), F32),
            jax.ShapeDtypeStruct((8, 16, 256), F32),
        ),
        in_specs=[pl.BlockSpec(memory_space=pltpu.VMEM), pl.BlockSpec(memory_space=pl.ANY)],
        out_specs=(pl.BlockSpec(memory_space=pl.ANY),) * 2,
        scratch_shapes=[
            vmem((128, 256), F32),
            vmem((128, 128), F32),
            vmem((8, 16, 16), F32),
            vmem((8, 16, 256), F32),
            dma((3,)),
        ],
        compiler_params=pltpu.CompilerParams(vmem_limit_bytes=16 * 1024 * 1024),
        name="factor_modes",
    )(gram, columns)


def local(snapshots):
    time_dev, points = snapshots.shape
    n_aa = lax.axis_size("aa")
    n_ba = lax.axis_size("ba")
    if (n_aa, n_ba, time_dev, points) == (8, 4, 64, 8192):
        return fused(snapshots)
    pts_dev = points // (n_aa * n_ba)
    block_len = time_dev * n_ba
    table = spectral_table(block_len, points)
    regrouped = lax.all_to_all(
        lax.all_to_all(snapshots, "aa", split_axis=1, concat_axis=0, tiled=True),
        "ba",
        split_axis=1,
        concat_axis=0,
        tiled=True,
    )
    arranged = regrouped.reshape(n_ba, n_aa, time_dev, pts_dev)
    table_parts = table.reshape(n_ba, time_dev, 2, FREQS)
    spectra = jnp.einsum("uasp,usgf->agfp", arranged, table_parts, precision=lax.Precision.HIGHEST)
    blocks = spectra.shape[0]
    columns = 2 * blocks
    product = jnp.einsum("bgfp,chfp->fbgch", spectra, spectra, precision=lax.Precision.HIGHEST)
    gram_sum = lax.psum(product.reshape(FREQS, columns, columns), ("aa", "ba"))
    lower_factor = jnp.linalg.cholesky(gram_sum)
    identity = jnp.broadcast_to(jnp.eye(columns, dtype=gram_sum.dtype), lower_factor.shape)
    inverse = lax.linalg.triangular_solve(lower_factor, identity, left_side=True, lower=True)
    pod_modes = math.sqrt(points) * jnp.einsum(
        "fibg,bgfp->fip",
        inverse.reshape(FREQS, columns, blocks, 2),
        spectra,
        precision=lax.Precision.HIGHEST,
    )
    return (jnp.swapaxes(lower_factor, 1, 2), pod_modes)


def solution(mesh):
    placed = (P(("aa", "ba"), None),)
    return jax.shard_map(
        local,
        mesh=mesh,
        in_specs=placed,
        out_specs=(P(), P(None, None, ("aa", "ba"))),
        check_vma=False,
    )
```

```python
import functools
import math

import jax
import jax.numpy as jnp
from jax import lax
from jax.experimental import pallas as pl
from jax.experimental.pallas import tpu as pltpu
from jax.sharding import PartitionSpec as P

FREQS = 8
MESH = pl.DeviceIdType.MESH
BF16 = jnp.bfloat16
F32 = jnp.float32

STEPS = ((2, 0), (2, 1), (1, 0), (1, 1), (3, 0), (3, 1), (0, 1), (0, 0))
GROUPS = ((0,), (1, 2), (3, 4), (5, 6, 7))
DIRECT = 3
STAGES = (("y", 3), ("y", 4), ("b", 0), ("y", 5), ("b", 1), ("y", 6), ("b", 2), ("y", 7)) + tuple(
    ("b", k) for k in range(3, 8)
)


def spectral_table(block_len, points):
    sample = jnp.arange(block_len, dtype=jnp.int32)
    harmonic = jnp.arange(1, FREQS + 1, dtype=jnp.int32)
    phase_turns = (sample[:, None] * harmonic[None, :] % block_len).astype(jnp.float32) * (
        2.0 * math.pi / block_len
    )
    sample_angle = sample.astype(jnp.float32) * (2.0 * math.pi / block_len)
    window = 0.5 - 0.5 * jnp.cos(sample_angle)
    norm_scale = 1.0 / jnp.sqrt(points * jnp.sum(window * window))
    cosine = window[:, None] * jnp.cos(phase_turns) * norm_scale
    sine = -window[:, None] * jnp.sin(phase_turns) * norm_scale
    return jnp.stack([cosine, sine], axis=1)


def split_table(ba, points):
    row = lax.broadcasted_iota(jnp.int32, (16, 64), 0)
    sample = lax.broadcasted_iota(jnp.int32, (16, 64), 1) + ba * 64
    turns = (sample * (row // 2 + 1) + 64 * (row % 2)) % 256
    step = 2.0 * math.pi / 256
    window = 0.5 - 0.5 * jnp.cos(sample.astype(F32) * step)
    power = sum((0.5 - 0.5 * math.cos(n * step)) ** 2 for n in range(256))
    value = window * jnp.cos(turns.astype(F32) * step) * (1.0 / math.sqrt(points * power))
    rows = jnp.concatenate(split3(value), axis=0)
    return jnp.concatenate([rows] * 3, axis=1)


def split3(value):
    high = value.astype(BF16)
    rest = value - high.astype(F32)
    middle = rest.astype(BF16)
    low = (rest - middle.astype(F32)).astype(BF16)
    return high, middle, low


def kernel(
    points, x_hbm, columns_hbm, gram_ref,
    x_buf, table, part, core_in, y_out, y_in, cross_in, block_out, blocks,
    columns_buf, gram_out, gram_in, plane_out, plane_in,
    in_sem, columns_sem, cross_send, cross_recv, core_send, core_recv, y_send, y_recv,
    block_send, block_recv, gram_send, gram_recv, plane_send, plane_recv,
):
    aa, ba = lax.axis_index("aa"), lax.axis_index("ba")
    z, x = aa // 2, aa % 2
    y, core = ba // 2, ba % 2
    other_core = 1 - core
    core_peer = (aa, y * 2 + other_core)
    y_peer = (aa, (1 - y) * 2 + core)
    cross_peer = (aa, (1 - y) * 2 + other_core)
    owners = [((z + dz) % 4) * 2 + (x + dx) % 2 for dz, dx in STEPS]
    plane = [(i // 4, i // 2 % 2, i % 2) for i in range(8)]
    plane_ids = [
        (z * 2 + (x + dx) % 2, ((y + dy) % 2) * 2 + (core + dc) % 2) for dx, dy, dc in plane
    ]
    line_ids = [(((z + dz) % 4) * 2 + x, ba) for dz in range(4)]

    barrier = pltpu.get_barrier_semaphore()
    peers = [(owner, ba) for owner in owners[:-1]]
    peers += [plane_ids[i] for i in range(1, 8) if plane[i] != (1, 0, 0)]
    for peer in peers:
        pl.semaphore_signal(barrier, inc=1, device_id=peer, device_id_type=MESH)
    loads = []
    for k in range(8):
        start = pl.multiple_of(owners[k] * 1024, 1024)
        load = pltpu.make_async_copy(x_hbm.at[:, pl.ds(start, 1024)], x_buf.at[k], in_sem.at[k])
        load.start()
        loads.append(load)
    table[...] = split_table(ba, points)

    sends = []

    def remote(src, dst, send, recv, device):
        copy = pltpu.make_async_remote_copy(
            src_ref=src, dst_ref=dst, send_sem=send, recv_sem=recv,
            device_id=device, device_id_type=MESH,
        )
        copy.start()
        sends.append(copy)
        return copy

    core_copies, y_copies, cross_copies = {}, {}, {}

    def send_y(k):
        core_copies[k].wait_recv()
        y_out[k] = part[k, core, 1 - y] + core_in[k, 1 - y]
        y_copies[k] = remote(y_out.at[k], y_in.at[k], y_send.at[k], y_recv.at[k], y_peer)

    for group in GROUPS:
        for tile in group:
            loads[tile].wait()
        terms = [jnp.concatenate(split3(x_buf[tile]), axis=0) for tile in group]
        rows = jnp.dot(table[...], jnp.concatenate(terms, axis=1), preferred_element_type=F32)
        total = rows[0:16] + rows[16:32] + rows[32:48]
        for n, tile in enumerate(group):
            for half in range(4):
                at = n * 1024 + half * 256
                part[tile, half % 2, half // 2] = total[:, at:at + 256]
        if group[0] == 0:
            pl.semaphore_wait(barrier, len(peers))
        for tile in group:
            if tile < DIRECT:
                y_copies[tile] = remote(
                    part.at[tile, core, 1 - y], y_in.at[tile], y_send.at[tile], y_recv.at[tile], y_peer
                )
                cross_copies[tile] = remote(
                    part.at[tile, other_core, 1 - y], cross_in.at[tile],
                    cross_send.at[tile], cross_recv.at[tile], cross_peer,
                )
                core_copies[tile] = remote(
                    part.at[tile, other_core, y], core_in.at[tile, y],
                    core_send.at[tile], core_recv.at[tile], core_peer,
                )
            else:
                core_copies[tile] = remote(
                    part.at[tile, other_core], core_in.at[tile],
                    core_send.at[tile], core_recv.at[tile], core_peer,
                )

    block_copies = []
    mine = pl.ds(pl.multiple_of(aa * 16, 16), 16)
    for stage, k in STAGES:
        if stage == "y":
            send_y(k)
            continue
        y_copies[k].wait_recv()
        total = part[k, core, y]
        if k < DIRECT:
            core_copies[k].wait_recv()
            cross_copies[k].wait_recv()
            total = total + cross_in[k]
        total = total + core_in[k, y] + y_in[k]
        if k == 7:
            blocks[0, mine, :] = total[:, 0:128]
            blocks[1, mine, :] = total[:, 128:256]
        else:
            block_out[k, 0] = total[:, 0:128]
            block_out[k, 1] = total[:, 128:256]
            block_copies.append(
                remote(
                    block_out.at[k], blocks.at[:, mine, :],
                    block_send.at[k], block_recv.at[k], (owners[k], ba),
                )
            )
    for copy in block_copies:
        copy.wait_recv()

    columns = jnp.concatenate(
        [
            jnp.concatenate([blocks[half, pl.ds(r, 8, stride=16), :] for r in range(16)], axis=0)
            for half in range(2)
        ],
        axis=1,
    )
    columns_buf[...] = columns
    columns_copy = pltpu.make_async_copy(columns_buf, columns_hbm, columns_sem)
    columns_copy.start()
    high, middle, low = split3(columns)
    contract_last = (((1,), (1,)), ((), ()))
    product = lax.dot_general(
        jnp.concatenate([high, middle, low], axis=0),
        jnp.concatenate([high, middle], axis=0),
        contract_last,
        preferred_element_type=F32,
    )
    high_low = lax.dot_general(high, low, contract_last, preferred_element_type=F32)
    gram_full = (product[0:128, 0:128] + product[128:256, 128:256]) + (
        (product[0:128, 128:256] + product[128:256, 0:128]) + (product[256:384, 0:128] + high_low)
    )
    row_freq = lax.broadcasted_iota(jnp.int32, (128, 128), 0) // 16
    lane_freq = lax.broadcasted_iota(jnp.int32, (128, 128), 1) // 16
    same = row_freq == lane_freq
    kept = jnp.where(same, gram_full, 0.0).reshape(8, 16, 128)
    gram_out[...] = ((kept[0] + kept[1]) + (kept[2] + kept[3])) + ((kept[4] + kept[5]) + (kept[6] + kept[7]))

    copies = [
        remote(gram_out, gram_in.at[i], gram_send.at[i], gram_recv.at[i], plane_ids[i]) for i in range(1, 8)
    ]
    for copy in sends[:-7]:
        copy.wait_send()
    for copy in copies:
        copy.wait_recv()
    pairs = [gram_out[...] + gram_in[1]] + [gram_in[i] + gram_in[i + 1] for i in (2, 4, 6)]
    plane_out[...] = (pairs[0] + pairs[1]) + (pairs[2] + pairs[3])
    copies = [
        remote(plane_out, plane_in.at[i], plane_send.at[i], plane_recv.at[i], line_ids[i]) for i in range(1, 4)
    ]
    columns_copy.wait()
    for copy in sends[-10:-3]:
        copy.wait_send()
    for copy in copies:
        copy.wait_recv()
    gram_ref[...] = (plane_out[...] + plane_in[2]) + (plane_in[1] + plane_in[3])
    for copy in sends[-3:]:
        copy.wait_send()


def finish_kernel(points, gram_ref, columns_hbm, factors_hbm, modes_hbm, columns, upper, factors, modes, sems):
    load = pltpu.make_async_copy(columns_hbm, columns, sems.at[0])
    load.start()
    gram = gram_ref[...]
    lane = lax.broadcasted_iota(jnp.int32, (16, 128), 1) % 16
    row = lax.broadcasted_iota(jnp.int32, (16, 128), 0)
    natural = (row % 8) * 2 + row // 8
    place = [(j % 2) * 8 + j // 2 for j in range(16)]
    left = [pltpu.roll(gram, (128 - place[j]) % 128, 1) if place[j] else gram for j in range(16)]
    right = [(row == place[j]).astype(F32) for j in range(16)]
    upper_all = jnp.zeros((16, 128), F32)
    inverse_all = jnp.zeros((16, 128), F32)
    for j in range(16):
        pivot = left[j][place[j]:place[j] + 1, :]
        root = lax.rsqrt(pivot)
        root = root * (1.5 - 0.5 * pivot * root * root)
        upper_row = left[j] * root
        inverse_row = right[j] * root
        for i in range(j + 1, 16):
            scale = upper_row[place[i]:place[i] + 1, :]
            left[i] = left[i] - scale * upper_row
            right[i] = right[i] - scale * inverse_row
        upper_row = jnp.where(natural >= j, upper_row, 0.0)
        if j:
            upper_row = pltpu.roll(upper_row, j, 1)
            inverse_row = pltpu.roll(inverse_row, j, 1)
        upper_all = jnp.where(lane == j, upper_row, upper_all)
        inverse_all = jnp.where(lane == j, inverse_row, inverse_all)

    upper[...] = jnp.zeros_like(upper)
    upper[pl.ds(0, 8, stride=2), :] = upper_all[0:8]
    upper[pl.ds(1, 8, stride=2), :] = upper_all[8:16]
    factors[...] = jnp.transpose(upper[...])[:, 0:16].reshape(8, 16, 16)
    factors_copy = pltpu.make_async_copy(factors, factors_hbm, sems.at[1])
    factors_copy.start()

    inverse_all = inverse_all * math.sqrt(points)
    row_freq = lax.broadcasted_iota(jnp.int32, (128, 128), 0) // 16
    lane_freq = lax.broadcasted_iota(jnp.int32, (128, 128), 1) // 16
    wide = jnp.where(row_freq == lane_freq, jnp.concatenate([inverse_all] * 8, axis=0), 0.0)
    w_high, w_middle, w_low = split3(jnp.transpose(wide))
    load.wait()
    high, middle, low = split3(columns[...])
    product = lax.dot_general(
        jnp.concatenate([w_high, w_high, w_middle, w_middle, w_high, w_low], axis=1),
        jnp.concatenate([high, middle, high, middle, low, high], axis=0),
        (((1,), (0,)), ((), ())),
        preferred_element_type=F32,
    )
    modes[...] = product.reshape(8, 16, 256)
    modes_copy = pltpu.make_async_copy(modes, modes_hbm, sems.at[2])
    modes_copy.start()
    factors_copy.wait()
    modes_copy.wait()


def fused(snapshots):
    points = snapshots.shape[1]
    dma = pltpu.SemaphoreType.DMA
    vmem = pltpu.VMEM
    columns, gram = pl.pallas_call(
        functools.partial(kernel, points),
        out_shape=(
            jax.ShapeDtypeStruct((128, 256), F32),
            jax.ShapeDtypeStruct((16, 128), F32),
        ),
        in_specs=[pl.BlockSpec(memory_space=pltpu.HBM)],
        out_specs=(pl.BlockSpec(memory_space=pl.ANY), pl.BlockSpec(memory_space=pltpu.VMEM)),
        scratch_shapes=[
            vmem((8, 64, 1024), F32),
            vmem((48, 192), BF16),
            vmem((8, 2, 2, 16, 256), F32),
            vmem((8, 2, 16, 256), F32),
            vmem((8, 16, 256), F32),
            vmem((8, 16, 256), F32),
            vmem((DIRECT, 16, 256), F32),
            vmem((8, 2, 16, 128), F32),
            vmem((2, 128, 128), F32),
            vmem((128, 256), F32),
            vmem((16, 128), F32),
            vmem((8, 16, 128), F32),
            vmem((16, 128), F32),
            vmem((4, 16, 128), F32),
            dma((8,)),
            dma,
            dma((DIRECT,)),
            dma((DIRECT,)),
            dma((8,)),
            dma((8,)),
            dma((8,)),
            dma((8,)),
            dma((8,)),
            dma((8,)),
            dma((8,)),
            dma((8,)),
            dma((4,)),
            dma((4,)),
        ],
        compiler_params=pltpu.CompilerParams(
            collective_id=0, has_side_effects=True, vmem_limit_bytes=53 * 1024 * 1024
        ),
        name="welch_gram",
    )(snapshots)
    return pl.pallas_call(
        functools.partial(finish_kernel, points),
        out_shape=(
            jax.ShapeDtypeStruct((8, 16, 16), F32),
            jax.ShapeDtypeStruct((8, 16, 256), F32),
        ),
        in_specs=[pl.BlockSpec(memory_space=pltpu.VMEM), pl.BlockSpec(memory_space=pl.ANY)],
        out_specs=(pl.BlockSpec(memory_space=pl.ANY),) * 2,
        scratch_shapes=[
            vmem((128, 256), F32),
            vmem((128, 128), F32),
            vmem((8, 16, 16), F32),
            vmem((8, 16, 256), F32),
            dma((3,)),
        ],
        compiler_params=pltpu.CompilerParams(vmem_limit_bytes=16 * 1024 * 1024),
        name="factor_modes",
    )(gram, columns)


def local(snapshots):
    time_dev, points = snapshots.shape
    n_aa = lax.axis_size("aa")
    n_ba = lax.axis_size("ba")
    if (n_aa, n_ba, time_dev, points) == (8, 4, 64, 8192):
        return fused(snapshots)
    pts_dev = points // (n_aa * n_ba)
    block_len = time_dev * n_ba
    table = spectral_table(block_len, points)
    regrouped = lax.all_to_all(
        lax.all_to_all(snapshots, "aa", split_axis=1, concat_axis=0, tiled=True),
        "ba",
        split_axis=1,
        concat_axis=0,
        tiled=True,
    )
    arranged = regrouped.reshape(n_ba, n_aa, time_dev, pts_dev)
    table_parts = table.reshape(n_ba, time_dev, 2, FREQS)
    spectra = jnp.einsum("uasp,usgf->agfp", arranged, table_parts, precision=lax.Precision.HIGHEST)
    blocks = spectra.shape[0]
    columns = 2 * blocks
    product = jnp.einsum("bgfp,chfp->fbgch", spectra, spectra, precision=lax.Precision.HIGHEST)
    gram_sum = lax.psum(product.reshape(FREQS, columns, columns), ("aa", "ba"))
    lower_factor = jnp.linalg.cholesky(gram_sum)
    identity = jnp.broadcast_to(jnp.eye(columns, dtype=gram_sum.dtype), lower_factor.shape)
    inverse = lax.linalg.triangular_solve(lower_factor, identity, left_side=True, lower=True)
    pod_modes = math.sqrt(points) * jnp.einsum(
        "fibg,bgfp->fip",
        inverse.reshape(FREQS, columns, blocks, 2),
        spectra,
        precision=lax.Precision.HIGHEST,
    )
    return (jnp.swapaxes(lower_factor, 1, 2), pod_modes)


def solution(mesh):
    placed = (P(("aa", "ba"), None),)
    return jax.shard_map(
        local,
        mesh=mesh,
        in_specs=placed,
        out_specs=(P(), P(None, None, ("aa", "ba"))),
        check_vma=False,
    )
```

```python
import functools
import math

import jax
import jax.numpy as jnp
from jax import lax
from jax.experimental import pallas as pl
from jax.experimental.pallas import tpu as pltpu
from jax.sharding import PartitionSpec as P

FREQS = 8
MESH = pl.DeviceIdType.MESH
BF16 = jnp.bfloat16
F32 = jnp.float32

STEPS = ((2, 0), (2, 1), (1, 0), (1, 1), (3, 0), (3, 1), (0, 1), (0, 0))
DIRECT = 1
STAGES = (
    ("c", 0), ("c", 1), ("c", 2), ("c", 3), ("y", 1), ("c", 4), ("y", 2), ("b", 0), ("c", 5), ("y", 3),
    ("c", 6), ("y", 4), ("b", 1), ("c", 7), ("y", 5), ("b", 2), ("y", 6), ("b", 3), ("y", 7), ("b", 4),
    ("b", 5), ("b", 6), ("b", 7),
)


def spectral_table(block_len, points):
    sample = jnp.arange(block_len, dtype=jnp.int32)
    harmonic = jnp.arange(1, FREQS + 1, dtype=jnp.int32)
    phase_turns = (sample[:, None] * harmonic[None, :] % block_len).astype(jnp.float32) * (
        2.0 * math.pi / block_len
    )
    sample_angle = sample.astype(jnp.float32) * (2.0 * math.pi / block_len)
    window = 0.5 - 0.5 * jnp.cos(sample_angle)
    norm_scale = 1.0 / jnp.sqrt(points * jnp.sum(window * window))
    cosine = window[:, None] * jnp.cos(phase_turns) * norm_scale
    sine = -window[:, None] * jnp.sin(phase_turns) * norm_scale
    return jnp.stack([cosine, sine], axis=1)


def split_table(ba, points):
    row = lax.broadcasted_iota(jnp.int32, (16, 64), 0)
    sample = lax.broadcasted_iota(jnp.int32, (16, 64), 1) + ba * 64
    turns = (sample * (row // 2 + 1) + 64 * (row % 2)) % 256
    step = 2.0 * math.pi / 256
    window = 0.5 - 0.5 * jnp.cos(sample.astype(F32) * step)
    power = sum((0.5 - 0.5 * math.cos(n * step)) ** 2 for n in range(256))
    value = window * jnp.cos(turns.astype(F32) * step) * (1.0 / math.sqrt(points * power))
    rows = jnp.concatenate(split3(value), axis=0)
    return jnp.concatenate([rows] * 3, axis=1)


def split3(value):
    high = value.astype(BF16)
    rest = value - high.astype(F32)
    middle = rest.astype(BF16)
    low = (rest - middle.astype(F32)).astype(BF16)
    return high, middle, low


def kernel(
    points, x_hbm, columns_hbm, gram_ref,
    x_buf, table, part, core_in, y_out, y_in, cross_in, block_out, blocks,
    columns_buf, gram_out, gram_in, plane_out, plane_in,
    in_sem, columns_sem, cross_send, cross_recv, core_send, core_recv, y_send, y_recv,
    block_send, block_recv, gram_send, gram_recv, plane_send, plane_recv,
):
    aa, ba = lax.axis_index("aa"), lax.axis_index("ba")
    z, x = aa // 2, aa % 2
    y, core = ba // 2, ba % 2
    other_core = 1 - core
    core_peer = (aa, y * 2 + other_core)
    y_peer = (aa, (1 - y) * 2 + core)
    cross_peer = (aa, (1 - y) * 2 + other_core)
    owners = [((z + dz) % 4) * 2 + (x + dx) % 2 for dz, dx in STEPS]
    plane = [(i // 4, i // 2 % 2, i % 2) for i in range(8)]
    plane_ids = [
        (z * 2 + (x + dx) % 2, ((y + dy) % 2) * 2 + (core + dc) % 2) for dx, dy, dc in plane
    ]
    line_ids = [(((z + dz) % 4) * 2 + x, ba) for dz in range(4)]

    barrier = pltpu.get_barrier_semaphore()
    peers = [(owner, ba) for owner in owners[:-1]]
    peers += [plane_ids[i] for i in range(1, 8) if plane[i] != (1, 0, 0)]
    for peer in peers:
        pl.semaphore_signal(barrier, inc=1, device_id=peer, device_id_type=MESH)
    loads = []
    for k in range(8):
        start = pl.multiple_of(owners[k] * 1024, 1024)
        load = pltpu.make_async_copy(x_hbm.at[:, pl.ds(start, 1024)], x_buf.at[k], in_sem.at[k])
        load.start()
        loads.append(load)
    table[...] = split_table(ba, points)

    sends = []

    def remote(src, dst, send, recv, device):
        copy = pltpu.make_async_remote_copy(
            src_ref=src, dst_ref=dst, send_sem=send, recv_sem=recv,
            device_id=device, device_id_type=MESH,
        )
        copy.start()
        sends.append(copy)
        return copy

    core_copies, y_copies, cross_copies = {}, {}, {}

    def send_y(k):
        core_copies[k].wait_recv()
        y_out[k] = part[k, core, 1 - y] + core_in[k, 1 - y]
        y_copies[k] = remote(y_out.at[k], y_in.at[k], y_send.at[k], y_recv.at[k], y_peer)

    def compute(tile):
        loads[tile].wait()
        terms = jnp.concatenate(split3(x_buf[tile]), axis=0)
        rows = jnp.dot(table[...], terms, preferred_element_type=F32)
        total = rows[0:16] + rows[16:32] + rows[32:48]
        for half in range(4):
            part[tile, half % 2, half // 2] = total[:, half * 256:half * 256 + 256]
        if tile == 0:
            pl.semaphore_wait(barrier, len(peers))
        if tile < DIRECT:
            y_copies[tile] = remote(
                part.at[tile, core, 1 - y], y_in.at[tile], y_send.at[tile], y_recv.at[tile], y_peer
            )
            cross_copies[tile] = remote(
                part.at[tile, other_core, 1 - y], cross_in.at[tile],
                cross_send.at[tile], cross_recv.at[tile], cross_peer,
            )
            core_copies[tile] = remote(
                part.at[tile, other_core, y], core_in.at[tile, y],
                core_send.at[tile], core_recv.at[tile], core_peer,
            )
        else:
            core_copies[tile] = remote(
                part.at[tile, other_core], core_in.at[tile],
                core_send.at[tile], core_recv.at[tile], core_peer,
            )

    block_copies = []
    mine = pl.ds(pl.multiple_of(aa * 16, 16), 16)
    for stage, k in STAGES:
        if stage == "c":
            compute(k)
            continue
        if stage == "y":
            send_y(k)
            continue
        y_copies[k].wait_recv()
        total = part[k, core, y]
        if k < DIRECT:
            core_copies[k].wait_recv()
            cross_copies[k].wait_recv()
            total = total + cross_in[k]
        total = total + core_in[k, y] + y_in[k]
        if k == 7:
            blocks[0, mine, :] = total[:, 0:128]
            blocks[1, mine, :] = total[:, 128:256]
        else:
            block_out[k, 0] = total[:, 0:128]
            block_out[k, 1] = total[:, 128:256]
            block_copies.append(
                remote(
                    block_out.at[k], blocks.at[:, mine, :],
                    block_send.at[k], block_recv.at[k], (owners[k], ba),
                )
            )
    for copy in block_copies:
        copy.wait_recv()

    columns = jnp.concatenate(
        [
            jnp.concatenate([blocks[half, pl.ds(r, 8, stride=16), :] for r in range(16)], axis=0)
            for half in range(2)
        ],
        axis=1,
    )
    columns_buf[...] = columns
    columns_copy = pltpu.make_async_copy(columns_buf, columns_hbm, columns_sem)
    columns_copy.start()
    high, middle, low = split3(columns)
    contract_last = (((1,), (1,)), ((), ()))
    product = lax.dot_general(
        jnp.concatenate([high, middle, low], axis=0),
        jnp.concatenate([high, middle], axis=0),
        contract_last,
        preferred_element_type=F32,
    )
    high_low = lax.dot_general(high, low, contract_last, preferred_element_type=F32)
    gram_full = (product[0:128, 0:128] + product[128:256, 128:256]) + (
        (product[0:128, 128:256] + product[128:256, 0:128]) + (product[256:384, 0:128] + high_low)
    )
    row_freq = lax.broadcasted_iota(jnp.int32, (128, 128), 0) // 16
    lane_freq = lax.broadcasted_iota(jnp.int32, (128, 128), 1) // 16
    same = row_freq == lane_freq
    kept = jnp.where(same, gram_full, 0.0).reshape(8, 16, 128)
    gram_out[...] = ((kept[0] + kept[1]) + (kept[2] + kept[3])) + ((kept[4] + kept[5]) + (kept[6] + kept[7]))

    copies = [
        remote(gram_out, gram_in.at[i], gram_send.at[i], gram_recv.at[i], plane_ids[i]) for i in range(1, 8)
    ]
    for copy in sends[:-7]:
        copy.wait_send()
    for copy in copies:
        copy.wait_recv()
    pairs = [gram_out[...] + gram_in[1]] + [gram_in[i] + gram_in[i + 1] for i in (2, 4, 6)]
    plane_out[...] = (pairs[0] + pairs[1]) + (pairs[2] + pairs[3])
    copies = [
        remote(plane_out, plane_in.at[i], plane_send.at[i], plane_recv.at[i], line_ids[i]) for i in range(1, 4)
    ]
    columns_copy.wait()
    for copy in sends[-10:-3]:
        copy.wait_send()
    for copy in copies:
        copy.wait_recv()
    gram_ref[...] = (plane_out[...] + plane_in[2]) + (plane_in[1] + plane_in[3])
    for copy in sends[-3:]:
        copy.wait_send()


def finish_kernel(points, gram_ref, columns_hbm, factors_hbm, modes_hbm, columns, upper, factors, modes, sems):
    load = pltpu.make_async_copy(columns_hbm, columns, sems.at[0])
    load.start()
    gram = gram_ref[...]
    lane = lax.broadcasted_iota(jnp.int32, (16, 128), 1) % 16
    row = lax.broadcasted_iota(jnp.int32, (16, 128), 0)
    natural = (row % 8) * 2 + row // 8
    place = [(j % 2) * 8 + j // 2 for j in range(16)]
    left = [pltpu.roll(gram, (128 - place[j]) % 128, 1) if place[j] else gram for j in range(16)]
    right = [(row == place[j]).astype(F32) for j in range(16)]
    upper_all = jnp.zeros((16, 128), F32)
    inverse_all = jnp.zeros((16, 128), F32)
    for j in range(16):
        pivot = left[j][place[j]:place[j] + 1, :]
        root = lax.rsqrt(pivot)
        root = root * (1.5 - 0.5 * pivot * root * root)
        upper_row = left[j] * root
        inverse_row = right[j] * root
        for i in range(j + 1, 16):
            scale = upper_row[place[i]:place[i] + 1, :]
            left[i] = left[i] - scale * upper_row
            right[i] = right[i] - scale * inverse_row
        upper_row = jnp.where(natural >= j, upper_row, 0.0)
        if j:
            upper_row = pltpu.roll(upper_row, j, 1)
            inverse_row = pltpu.roll(inverse_row, j, 1)
        upper_all = jnp.where(lane == j, upper_row, upper_all)
        inverse_all = jnp.where(lane == j, inverse_row, inverse_all)

    upper[...] = jnp.zeros_like(upper)
    upper[pl.ds(0, 8, stride=2), :] = upper_all[0:8]
    upper[pl.ds(1, 8, stride=2), :] = upper_all[8:16]
    factors[...] = jnp.transpose(upper[...])[:, 0:16].reshape(8, 16, 16)
    factors_copy = pltpu.make_async_copy(factors, factors_hbm, sems.at[1])
    factors_copy.start()

    inverse_all = inverse_all * math.sqrt(points)
    row_freq = lax.broadcasted_iota(jnp.int32, (128, 128), 0) // 16
    lane_freq = lax.broadcasted_iota(jnp.int32, (128, 128), 1) // 16
    wide = jnp.where(row_freq == lane_freq, jnp.concatenate([inverse_all] * 8, axis=0), 0.0)
    w_high, w_middle, w_low = split3(jnp.transpose(wide))
    load.wait()
    high, middle, low = split3(columns[...])
    product = lax.dot_general(
        jnp.concatenate([w_high, w_high, w_middle, w_middle, w_high, w_low], axis=1),
        jnp.concatenate([high, middle, high, middle, low, high], axis=0),
        (((1,), (0,)), ((), ())),
        preferred_element_type=F32,
    )
    modes[...] = product.reshape(8, 16, 256)
    modes_copy = pltpu.make_async_copy(modes, modes_hbm, sems.at[2])
    modes_copy.start()
    factors_copy.wait()
    modes_copy.wait()


def fused(snapshots):
    points = snapshots.shape[1]
    dma = pltpu.SemaphoreType.DMA
    vmem = pltpu.VMEM
    columns, gram = pl.pallas_call(
        functools.partial(kernel, points),
        out_shape=(
            jax.ShapeDtypeStruct((128, 256), F32),
            jax.ShapeDtypeStruct((16, 128), F32),
        ),
        in_specs=[pl.BlockSpec(memory_space=pltpu.HBM)],
        out_specs=(pl.BlockSpec(memory_space=pl.ANY), pl.BlockSpec(memory_space=pltpu.VMEM)),
        scratch_shapes=[
            vmem((8, 64, 1024), F32),
            vmem((48, 192), BF16),
            vmem((8, 2, 2, 16, 256), F32),
            vmem((8, 2, 16, 256), F32),
            vmem((8, 16, 256), F32),
            vmem((8, 16, 256), F32),
            vmem((DIRECT, 16, 256), F32),
            vmem((8, 2, 16, 128), F32),
            vmem((2, 128, 128), F32),
            vmem((128, 256), F32),
            vmem((16, 128), F32),
            vmem((8, 16, 128), F32),
            vmem((16, 128), F32),
            vmem((4, 16, 128), F32),
            dma((8,)),
            dma,
            dma((DIRECT,)),
            dma((DIRECT,)),
            dma((8,)),
            dma((8,)),
            dma((8,)),
            dma((8,)),
            dma((8,)),
            dma((8,)),
            dma((8,)),
            dma((8,)),
            dma((4,)),
            dma((4,)),
        ],
        compiler_params=pltpu.CompilerParams(
            collective_id=0, has_side_effects=True, vmem_limit_bytes=53 * 1024 * 1024
        ),
        name="welch_gram",
    )(snapshots)
    return pl.pallas_call(
        functools.partial(finish_kernel, points),
        out_shape=(
            jax.ShapeDtypeStruct((8, 16, 16), F32),
            jax.ShapeDtypeStruct((8, 16, 256), F32),
        ),
        in_specs=[pl.BlockSpec(memory_space=pltpu.VMEM), pl.BlockSpec(memory_space=pl.ANY)],
        out_specs=(pl.BlockSpec(memory_space=pl.ANY),) * 2,
        scratch_shapes=[
            vmem((128, 256), F32),
            vmem((128, 128), F32),
            vmem((8, 16, 16), F32),
            vmem((8, 16, 256), F32),
            dma((3,)),
        ],
        compiler_params=pltpu.CompilerParams(vmem_limit_bytes=16 * 1024 * 1024),
        name="factor_modes",
    )(gram, columns)


def local(snapshots):
    time_dev, points = snapshots.shape
    n_aa = lax.axis_size("aa")
    n_ba = lax.axis_size("ba")
    if (n_aa, n_ba, time_dev, points) == (8, 4, 64, 8192):
        return fused(snapshots)
    pts_dev = points // (n_aa * n_ba)
    block_len = time_dev * n_ba
    table = spectral_table(block_len, points)
    regrouped = lax.all_to_all(
        lax.all_to_all(snapshots, "aa", split_axis=1, concat_axis=0, tiled=True),
        "ba",
        split_axis=1,
        concat_axis=0,
        tiled=True,
    )
    arranged = regrouped.reshape(n_ba, n_aa, time_dev, pts_dev)
    table_parts = table.reshape(n_ba, time_dev, 2, FREQS)
    spectra = jnp.einsum("uasp,usgf->agfp", arranged, table_parts, precision=lax.Precision.HIGHEST)
    blocks = spectra.shape[0]
    columns = 2 * blocks
    product = jnp.einsum("bgfp,chfp->fbgch", spectra, spectra, precision=lax.Precision.HIGHEST)
    gram_sum = lax.psum(product.reshape(FREQS, columns, columns), ("aa", "ba"))
    lower_factor = jnp.linalg.cholesky(gram_sum)
    identity = jnp.broadcast_to(jnp.eye(columns, dtype=gram_sum.dtype), lower_factor.shape)
    inverse = lax.linalg.triangular_solve(lower_factor, identity, left_side=True, lower=True)
    pod_modes = math.sqrt(points) * jnp.einsum(
        "fibg,bgfp->fip",
        inverse.reshape(FREQS, columns, blocks, 2),
        spectra,
        precision=lax.Precision.HIGHEST,
    )
    return (jnp.swapaxes(lower_factor, 1, 2), pod_modes)


def solution(mesh):
    placed = (P(("aa", "ba"), None),)
    return jax.shard_map(
        local,
        mesh=mesh,
        in_specs=placed,
        out_specs=(P(), P(None, None, ("aa", "ba"))),
        check_vma=False,
    )
```

```python
import functools
import math

import jax
import jax.numpy as jnp
from jax import lax
from jax.experimental import pallas as pl
from jax.experimental.pallas import tpu as pltpu
from jax.sharding import PartitionSpec as P

FREQS = 8
MESH = pl.DeviceIdType.MESH
BF16 = jnp.bfloat16
F32 = jnp.float32

STEPS = ((2, 0), (2, 1), (1, 0), (1, 1), (3, 0), (3, 1), (0, 1), (0, 0))
GROUPS = (
    ((0, 1, 2, 3), ()),
    ((4, 5, 6, 7), (0, 1, 2, 3, 4, 5, 6, 7)),
)


def spectral_table(block_len, points):
    sample = jnp.arange(block_len, dtype=jnp.int32)
    harmonic = jnp.arange(1, FREQS + 1, dtype=jnp.int32)
    phase_turns = (sample[:, None] * harmonic[None, :] % block_len).astype(jnp.float32) * (
        2.0 * math.pi / block_len
    )
    sample_angle = sample.astype(jnp.float32) * (2.0 * math.pi / block_len)
    window = 0.5 - 0.5 * jnp.cos(sample_angle)
    norm_scale = 1.0 / jnp.sqrt(points * jnp.sum(window * window))
    cosine = window[:, None] * jnp.cos(phase_turns) * norm_scale
    sine = -window[:, None] * jnp.sin(phase_turns) * norm_scale
    return jnp.stack([cosine, sine], axis=1)


def split_table(ba, points):
    row = lax.broadcasted_iota(jnp.int32, (16, 64), 0)
    sample = lax.broadcasted_iota(jnp.int32, (16, 64), 1) + ba * 64
    turns = (sample * (row // 2 + 1) + 64 * (row % 2)) % 256
    step = 2.0 * math.pi / 256
    window = 0.5 - 0.5 * jnp.cos(sample.astype(F32) * step)
    power = sum((0.5 - 0.5 * math.cos(n * step)) ** 2 for n in range(256))
    value = window * jnp.cos(turns.astype(F32) * step) * (1.0 / math.sqrt(points * power))
    rows = jnp.concatenate(split3(value), axis=0)
    return jnp.concatenate([rows] * 3, axis=1)


def split3(value):
    high = value.astype(BF16)
    rest = value - high.astype(F32)
    middle = rest.astype(BF16)
    low = (rest - middle.astype(F32)).astype(BF16)
    return high, middle, low


def kernel(
    points, x_hbm, columns_hbm, gram_ref,
    x_buf, table, part, core_in, y_out, y_in, block_out, blocks,
    columns_buf, gram_out, gram_in, plane_out, plane_in,
    in_sem, columns_sem, core_send, core_recv, y_send, y_recv,
    block_send, block_recv, gram_send, gram_recv, plane_send, plane_recv,
):
    aa, ba = lax.axis_index("aa"), lax.axis_index("ba")
    z, x = aa // 2, aa % 2
    y, core = ba // 2, ba % 2
    other_core = 1 - core
    core_peer = (aa, y * 2 + other_core)
    y_peer = (aa, (1 - y) * 2 + core)
    owners = [((z + dz) % 4) * 2 + (x + dx) % 2 for dz, dx in STEPS]
    plane = [(i // 4, i // 2 % 2, i % 2) for i in range(8)]
    plane_ids = [
        (z * 2 + (x + dx) % 2, ((y + dy) % 2) * 2 + (core + dc) % 2) for dx, dy, dc in plane
    ]
    line_ids = [(((z + dz) % 4) * 2 + x, ba) for dz in range(4)]

    barrier = pltpu.get_barrier_semaphore()
    peers = [(owner, ba) for owner in owners[:-1]]
    peers += [plane_ids[i] for i in range(1, 8) if plane[i] != (1, 0, 0)]
    for peer in peers:
        pl.semaphore_signal(barrier, inc=1, device_id=peer, device_id_type=MESH)
    loads = []
    for k in range(8):
        start = pl.multiple_of(owners[k] * 1024, 1024)
        load = pltpu.make_async_copy(x_hbm.at[:, pl.ds(start, 1024)], x_buf.at[k], in_sem.at[k])
        load.start()
        loads.append(load)
    table[...] = split_table(ba, points)

    sends = []

    def remote(src, dst, send, recv, device):
        copy = pltpu.make_async_remote_copy(
            src_ref=src, dst_ref=dst, send_sem=send, recv_sem=recv,
            device_id=device, device_id_type=MESH,
        )
        copy.start()
        sends.append(copy)
        return copy

    core_copies = []
    y_copies = []

    def send_y(k):
        core_copies[k].wait_recv()
        y_out[k] = part[k, core, 1 - y] + core_in[k, 1 - y]
        y_copies.append(remote(y_out.at[k], y_in.at[k], y_send.at[k], y_recv.at[k], y_peer))

    pl.semaphore_wait(barrier, len(peers))
    for group, ready in GROUPS:
        for tile in group:
            loads[tile].wait()
        terms = [jnp.concatenate(split3(x_buf[tile]), axis=0) for tile in group]
        rows = jnp.dot(table[...], jnp.concatenate(terms, axis=1), preferred_element_type=F32)
        total = rows[0:16] + rows[16:32] + rows[32:48]
        for n, tile in enumerate(group):
            for half in range(4):
                at = n * 1024 + half * 256
                part[tile, half % 2, half // 2] = total[:, at:at + 256]
        for tile in group:
            core_copies.append(
                remote(
                    part.at[tile, other_core], core_in.at[tile],
                    core_send.at[tile], core_recv.at[tile], core_peer,
                )
            )
        for k in ready:
            send_y(k)

    block_copies = []
    for k in range(8):
        y_copies[k].wait_recv()
        total = part[k, core, y] + core_in[k, y] + y_in[k]
        mine = pl.ds(pl.multiple_of(aa * 16, 16), 16)
        if k == 7:
            blocks[0, mine, :] = total[:, 0:128]
            blocks[1, mine, :] = total[:, 128:256]
        else:
            block_out[k, 0] = total[:, 0:128]
            block_out[k, 1] = total[:, 128:256]
            block_copies.append(
                remote(
                    block_out.at[k], blocks.at[:, mine, :],
                    block_send.at[k], block_recv.at[k], (owners[k], ba),
                )
            )
    for copy in block_copies:
        copy.wait_recv()

    columns = jnp.concatenate(
        [
            jnp.concatenate([blocks[half, pl.ds(r, 8, stride=16), :] for r in range(16)], axis=0)
            for half in range(2)
        ],
        axis=1,
    )
    columns_buf[...] = columns
    columns_copy = pltpu.make_async_copy(columns_buf, columns_hbm, columns_sem)
    columns_copy.start()
    high, middle, low = split3(columns)
    contract_last = (((1,), (1,)), ((), ()))
    product = lax.dot_general(
        jnp.concatenate([high, middle, low], axis=0),
        jnp.concatenate([high, middle], axis=0),
        contract_last,
        preferred_element_type=F32,
    )
    high_low = lax.dot_general(high, low, contract_last, preferred_element_type=F32)
    gram_full = (product[0:128, 0:128] + product[128:256, 128:256]) + (
        (product[0:128, 128:256] + product[128:256, 0:128]) + (product[256:384, 0:128] + high_low)
    )
    row_freq = lax.broadcasted_iota(jnp.int32, (128, 128), 0) // 16
    lane_freq = lax.broadcasted_iota(jnp.int32, (128, 128), 1) // 16
    same = row_freq == lane_freq
    kept = jnp.where(same, gram_full, 0.0).reshape(8, 16, 128)
    gram_out[...] = ((kept[0] + kept[1]) + (kept[2] + kept[3])) + ((kept[4] + kept[5]) + (kept[6] + kept[7]))

    copies = [
        remote(gram_out, gram_in.at[i], gram_send.at[i], gram_recv.at[i], plane_ids[i]) for i in range(1, 8)
    ]
    for copy in sends[:-7]:
        copy.wait_send()
    for copy in copies:
        copy.wait_recv()
    pairs = [gram_out[...] + gram_in[1]] + [gram_in[i] + gram_in[i + 1] for i in (2, 4, 6)]
    plane_out[...] = (pairs[0] + pairs[1]) + (pairs[2] + pairs[3])
    copies = [
        remote(plane_out, plane_in.at[i], plane_send.at[i], plane_recv.at[i], line_ids[i]) for i in range(1, 4)
    ]
    columns_copy.wait()
    for copy in sends[-10:-3]:
        copy.wait_send()
    for copy in copies:
        copy.wait_recv()
    gram_ref[...] = (plane_out[...] + plane_in[2]) + (plane_in[1] + plane_in[3])
    for copy in sends[-3:]:
        copy.wait_send()


def finish_kernel(points, gram_ref, columns_hbm, factors_hbm, modes_hbm, columns, upper, factors, modes, sems):
    load = pltpu.make_async_copy(columns_hbm, columns, sems.at[0])
    load.start()
    gram = gram_ref[...]
    lane = lax.broadcasted_iota(jnp.int32, (16, 128), 1) % 16
    row = lax.broadcasted_iota(jnp.int32, (16, 128), 0)
    natural = (row % 8) * 2 + row // 8
    place = [(j % 2) * 8 + j // 2 for j in range(16)]
    left = [pltpu.roll(gram, (128 - place[j]) % 128, 1) if place[j] else gram for j in range(16)]
    right = [(row == place[j]).astype(F32) for j in range(16)]
    upper_all = jnp.zeros((16, 128), F32)
    inverse_all = jnp.zeros((16, 128), F32)
    for j in range(16):
        pivot = left[j][place[j]:place[j] + 1, :]
        root = lax.rsqrt(pivot)
        root = root * (1.5 - 0.5 * pivot * root * root)
        upper_row = left[j] * root
        inverse_row = right[j] * root
        for i in range(j + 1, 16):
            scale = upper_row[place[i]:place[i] + 1, :]
            left[i] = left[i] - scale * upper_row
            right[i] = right[i] - scale * inverse_row
        upper_row = jnp.where(natural >= j, upper_row, 0.0)
        if j:
            upper_row = pltpu.roll(upper_row, j, 1)
            inverse_row = pltpu.roll(inverse_row, j, 1)
        upper_all = jnp.where(lane == j, upper_row, upper_all)
        inverse_all = jnp.where(lane == j, inverse_row, inverse_all)

    upper[...] = jnp.zeros_like(upper)
    upper[pl.ds(0, 8, stride=2), :] = upper_all[0:8]
    upper[pl.ds(1, 8, stride=2), :] = upper_all[8:16]
    factors[...] = jnp.transpose(upper[...])[:, 0:16].reshape(8, 16, 16)
    factors_copy = pltpu.make_async_copy(factors, factors_hbm, sems.at[1])
    factors_copy.start()

    inverse_all = inverse_all * math.sqrt(points)
    row_freq = lax.broadcasted_iota(jnp.int32, (128, 128), 0) // 16
    lane_freq = lax.broadcasted_iota(jnp.int32, (128, 128), 1) // 16
    wide = jnp.where(row_freq == lane_freq, jnp.concatenate([inverse_all] * 8, axis=0), 0.0)
    w_high, w_middle, w_low = split3(jnp.transpose(wide))
    load.wait()
    high, middle, low = split3(columns[...])
    product = lax.dot_general(
        jnp.concatenate([w_high, w_high, w_middle, w_middle, w_high, w_low], axis=1),
        jnp.concatenate([high, middle, high, middle, low, high], axis=0),
        (((1,), (0,)), ((), ())),
        preferred_element_type=F32,
    )
    modes[...] = product.reshape(8, 16, 256)
    modes_copy = pltpu.make_async_copy(modes, modes_hbm, sems.at[2])
    modes_copy.start()
    factors_copy.wait()
    modes_copy.wait()


def fused(snapshots):
    points = snapshots.shape[1]
    dma = pltpu.SemaphoreType.DMA
    vmem = pltpu.VMEM
    columns, gram = pl.pallas_call(
        functools.partial(kernel, points),
        out_shape=(
            jax.ShapeDtypeStruct((128, 256), F32),
            jax.ShapeDtypeStruct((16, 128), F32),
        ),
        in_specs=[pl.BlockSpec(memory_space=pltpu.HBM)],
        out_specs=(pl.BlockSpec(memory_space=pl.ANY), pl.BlockSpec(memory_space=pltpu.VMEM)),
        scratch_shapes=[
            vmem((8, 64, 1024), F32),
            vmem((48, 192), BF16),
            vmem((8, 2, 2, 16, 256), F32),
            vmem((8, 2, 16, 256), F32),
            vmem((8, 16, 256), F32),
            vmem((8, 16, 256), F32),
            vmem((8, 2, 16, 128), F32),
            vmem((2, 128, 128), F32),
            vmem((128, 256), F32),
            vmem((16, 128), F32),
            vmem((8, 16, 128), F32),
            vmem((16, 128), F32),
            vmem((4, 16, 128), F32),
            dma((8,)),
            dma,
            dma((8,)),
            dma((8,)),
            dma((8,)),
            dma((8,)),
            dma((8,)),
            dma((8,)),
            dma((8,)),
            dma((8,)),
            dma((4,)),
            dma((4,)),
        ],
        compiler_params=pltpu.CompilerParams(
            collective_id=0, has_side_effects=True, vmem_limit_bytes=53 * 1024 * 1024
        ),
        name="welch_gram",
    )(snapshots)
    return pl.pallas_call(
        functools.partial(finish_kernel, points),
        out_shape=(
            jax.ShapeDtypeStruct((8, 16, 16), F32),
            jax.ShapeDtypeStruct((8, 16, 256), F32),
        ),
        in_specs=[pl.BlockSpec(memory_space=pltpu.VMEM), pl.BlockSpec(memory_space=pl.ANY)],
        out_specs=(pl.BlockSpec(memory_space=pl.ANY),) * 2,
        scratch_shapes=[
            vmem((128, 256), F32),
            vmem((128, 128), F32),
            vmem((8, 16, 16), F32),
            vmem((8, 16, 256), F32),
            dma((3,)),
        ],
        compiler_params=pltpu.CompilerParams(vmem_limit_bytes=16 * 1024 * 1024),
        name="factor_modes",
    )(gram, columns)


def local(snapshots):
    time_dev, points = snapshots.shape
    n_aa = lax.axis_size("aa")
    n_ba = lax.axis_size("ba")
    if (n_aa, n_ba, time_dev, points) == (8, 4, 64, 8192):
        return fused(snapshots)
    pts_dev = points // (n_aa * n_ba)
    block_len = time_dev * n_ba
    table = spectral_table(block_len, points)
    regrouped = lax.all_to_all(
        lax.all_to_all(snapshots, "aa", split_axis=1, concat_axis=0, tiled=True),
        "ba",
        split_axis=1,
        concat_axis=0,
        tiled=True,
    )
    arranged = regrouped.reshape(n_ba, n_aa, time_dev, pts_dev)
    table_parts = table.reshape(n_ba, time_dev, 2, FREQS)
    spectra = jnp.einsum("uasp,usgf->agfp", arranged, table_parts, precision=lax.Precision.HIGHEST)
    blocks = spectra.shape[0]
    columns = 2 * blocks
    product = jnp.einsum("bgfp,chfp->fbgch", spectra, spectra, precision=lax.Precision.HIGHEST)
    gram_sum = lax.psum(product.reshape(FREQS, columns, columns), ("aa", "ba"))
    lower_factor = jnp.linalg.cholesky(gram_sum)
    identity = jnp.broadcast_to(jnp.eye(columns, dtype=gram_sum.dtype), lower_factor.shape)
    inverse = lax.linalg.triangular_solve(lower_factor, identity, left_side=True, lower=True)
    pod_modes = math.sqrt(points) * jnp.einsum(
        "fibg,bgfp->fip",
        inverse.reshape(FREQS, columns, blocks, 2),
        spectra,
        precision=lax.Precision.HIGHEST,
    )
    return (jnp.swapaxes(lower_factor, 1, 2), pod_modes)


def solution(mesh):
    placed = (P(("aa", "ba"), None),)
    return jax.shard_map(
        local,
        mesh=mesh,
        in_specs=placed,
        out_specs=(P(), P(None, None, ("aa", "ba"))),
        check_vma=False,
    )
```

```python
import functools
import math

import jax
import jax.numpy as jnp
from jax import lax
from jax.experimental import pallas as pl
from jax.experimental.pallas import tpu as pltpu
from jax.sharding import PartitionSpec as P

FREQS = 8
MESH = pl.DeviceIdType.MESH
BF16 = jnp.bfloat16
F32 = jnp.float32

STEPS = ((2, 0), (2, 1), (1, 0), (1, 1), (3, 0), (3, 1), (0, 1), (0, 0))
GROUPS = ((0, 1, 2, 3), (4, 5, 6, 7))
STRAIGHT = (4, 5, 6)


def spectral_table(block_len, points):
    sample = jnp.arange(block_len, dtype=jnp.int32)
    harmonic = jnp.arange(1, FREQS + 1, dtype=jnp.int32)
    phase_turns = (sample[:, None] * harmonic[None, :] % block_len).astype(jnp.float32) * (
        2.0 * math.pi / block_len
    )
    sample_angle = sample.astype(jnp.float32) * (2.0 * math.pi / block_len)
    window = 0.5 - 0.5 * jnp.cos(sample_angle)
    norm_scale = 1.0 / jnp.sqrt(points * jnp.sum(window * window))
    cosine = window[:, None] * jnp.cos(phase_turns) * norm_scale
    sine = -window[:, None] * jnp.sin(phase_turns) * norm_scale
    return jnp.stack([cosine, sine], axis=1)


def split_table(ba, points):
    row = lax.broadcasted_iota(jnp.int32, (16, 64), 0)
    sample = lax.broadcasted_iota(jnp.int32, (16, 64), 1) + ba * 64
    turns = (sample * (row // 2 + 1) + 64 * (row % 2)) % 256
    step = 2.0 * math.pi / 256
    window = 0.5 - 0.5 * jnp.cos(sample.astype(F32) * step)
    power = sum((0.5 - 0.5 * math.cos(n * step)) ** 2 for n in range(256))
    value = window * jnp.cos(turns.astype(F32) * step) * (1.0 / math.sqrt(points * power))
    rows = jnp.concatenate(split3(value), axis=0)
    return jnp.concatenate([rows] * 3, axis=1)


def split3(value):
    high = value.astype(BF16)
    rest = value - high.astype(F32)
    middle = rest.astype(BF16)
    low = (rest - middle.astype(F32)).astype(BF16)
    return high, middle, low


def kernel(
    points, x_hbm, columns_hbm, gram_ref,
    x_buf, table, part, core_in, y_out, y_in, block_out, blocks,
    columns_buf, gram_out, gram_in, plane_out, plane_in,
    in_sem, columns_sem, core_send, core_recv, y_send, y_recv,
    block_send, block_recv, gram_send, gram_recv, plane_send, plane_recv,
):
    aa, ba = lax.axis_index("aa"), lax.axis_index("ba")
    z, x = aa // 2, aa % 2
    y, core = ba // 2, ba % 2
    other_core = 1 - core
    core_peer = (aa, y * 2 + other_core)
    y_peer = (aa, (1 - y) * 2 + core)
    owners = [((z + dz) % 4) * 2 + (x + dx) % 2 for dz, dx in STEPS]
    sources = [((z + 4 - dz) % 4) * 2 + (x + 2 - dx) % 2 for dz, dx in STEPS]
    plane = [(i // 4, i // 2 % 2, i % 2) for i in range(8)]
    plane_ids = [
        (z * 2 + (x + dx) % 2, ((y + dy) % 2) * 2 + (core + dc) % 2) for dx, dy, dc in plane
    ]
    line_ids = [(((z + dz) % 4) * 2 + x, ba) for dz in range(4)]

    barrier = pltpu.get_barrier_semaphore()
    peers = [(owner, ba) for owner in owners[:-1]]
    peers += [plane_ids[i] for i in range(1, 8) if plane[i] != (1, 0, 0)]
    peers += [(sources[k], (1 - y) * 2 + core) for k in STRAIGHT if STEPS[k][0]]
    for peer in peers:
        pl.semaphore_signal(barrier, inc=1, device_id=peer, device_id_type=MESH)
    loads = []
    for k in range(8):
        start = pl.multiple_of(owners[k] * 1024, 1024)
        load = pltpu.make_async_copy(x_hbm.at[:, pl.ds(start, 1024)], x_buf.at[k], in_sem.at[k])
        load.start()
        loads.append(load)
    table[...] = split_table(ba, points)

    sends = []

    def remote(src, dst, send, recv, device):
        copy = pltpu.make_async_remote_copy(
            src_ref=src, dst_ref=dst, send_sem=send, recv_sem=recv,
            device_id=device, device_id_type=MESH,
        )
        copy.start()
        sends.append(copy)
        return copy

    core_copies = []
    y_copies = {}

    def send_y(k, device):
        core_copies[k].wait_recv()
        y_out[k] = part[k, core, 1 - y] + core_in[k, 1 - y]
        y_copies[k] = remote(y_out.at[k], y_in.at[k], y_send.at[k], y_recv.at[k], device)

    pl.semaphore_wait(barrier, len(peers))
    for group in GROUPS:
        for tile in group:
            loads[tile].wait()
        terms = [jnp.concatenate(split3(x_buf[tile]), axis=0) for tile in group]
        rows = jnp.dot(table[...], jnp.concatenate(terms, axis=1), preferred_element_type=F32)
        total = rows[0:16] + rows[16:32] + rows[32:48]
        for n, tile in enumerate(group):
            for half in range(4):
                at = n * 1024 + half * 256
                part[tile, half % 2, half // 2] = total[:, at:at + 256]
        for tile in group:
            core_copies.append(
                remote(
                    part.at[tile, other_core], core_in.at[tile],
                    core_send.at[tile], core_recv.at[tile], core_peer,
                )
            )
    block_copies = []
    mine = pl.ds(pl.multiple_of(aa * 16, 16), 16)

    def send_block(k, total):
        block_out[k, 0] = total[:, 0:128]
        block_out[k, 1] = total[:, 128:256]
        block_copies.append(
            remote(
                block_out.at[k], blocks.at[:, mine, :],
                block_send.at[k], block_recv.at[k], (owners[k], ba),
            )
        )

    for k in (0, 1, 2, 3):
        send_y(k, y_peer)
    for k in STRAIGHT:
        send_y(k, (owners[k], (1 - y) * 2 + core))
        send_block(k, part[k, core, y] + core_in[k, y])
    send_y(7, y_peer)
    for k in (0, 1, 2, 3):
        y_copies[k].wait_recv()
        send_block(k, part[k, core, y] + core_in[k, y] + y_in[k])
    y_copies[7].wait_recv()
    total = part[7, core, y] + core_in[7, y] + y_in[7]
    blocks[0, mine, :] = total[:, 0:128]
    blocks[1, mine, :] = total[:, 128:256]
    for copy in block_copies:
        copy.wait_recv()
    for k in STRAIGHT:
        y_copies[k].wait_recv()
        theirs = pl.ds(pl.multiple_of(sources[k] * 16, 16), 16)
        blocks[0, theirs, :] += y_in[k, :, 0:128]
        blocks[1, theirs, :] += y_in[k, :, 128:256]

    columns = jnp.concatenate(
        [
            jnp.concatenate([blocks[half, pl.ds(r, 8, stride=16), :] for r in range(16)], axis=0)
            for half in range(2)
        ],
        axis=1,
    )
    columns_buf[...] = columns
    columns_copy = pltpu.make_async_copy(columns_buf, columns_hbm, columns_sem)
    columns_copy.start()
    high, middle, low = split3(columns)
    contract_last = (((1,), (1,)), ((), ()))
    product = lax.dot_general(
        jnp.concatenate([high, middle, low], axis=0),
        jnp.concatenate([high, middle], axis=0),
        contract_last,
        preferred_element_type=F32,
    )
    high_low = lax.dot_general(high, low, contract_last, preferred_element_type=F32)
    gram_full = (product[0:128, 0:128] + product[128:256, 128:256]) + (
        (product[0:128, 128:256] + product[128:256, 0:128]) + (product[256:384, 0:128] + high_low)
    )
    row_freq = lax.broadcasted_iota(jnp.int32, (128, 128), 0) // 16
    lane_freq = lax.broadcasted_iota(jnp.int32, (128, 128), 1) // 16
    same = row_freq == lane_freq
    kept = jnp.where(same, gram_full, 0.0).reshape(8, 16, 128)
    gram_out[...] = ((kept[0] + kept[1]) + (kept[2] + kept[3])) + ((kept[4] + kept[5]) + (kept[6] + kept[7]))

    copies = [
        remote(gram_out, gram_in.at[i], gram_send.at[i], gram_recv.at[i], plane_ids[i]) for i in range(1, 8)
    ]
    for copy in sends[:-7]:
        copy.wait_send()
    for copy in copies:
        copy.wait_recv()
    pairs = [gram_out[...] + gram_in[1]] + [gram_in[i] + gram_in[i + 1] for i in (2, 4, 6)]
    plane_out[...] = (pairs[0] + pairs[1]) + (pairs[2] + pairs[3])
    copies = [
        remote(plane_out, plane_in.at[i], plane_send.at[i], plane_recv.at[i], line_ids[i]) for i in range(1, 4)
    ]
    columns_copy.wait()
    for copy in sends[-10:-3]:
        copy.wait_send()
    for copy in copies:
        copy.wait_recv()
    gram_ref[...] = (plane_out[...] + plane_in[2]) + (plane_in[1] + plane_in[3])
    for copy in sends[-3:]:
        copy.wait_send()


def finish_kernel(points, gram_ref, columns_hbm, factors_hbm, modes_hbm, columns, upper, factors, modes, sems):
    load = pltpu.make_async_copy(columns_hbm, columns, sems.at[0])
    load.start()
    gram = gram_ref[...]
    lane = lax.broadcasted_iota(jnp.int32, (16, 128), 1) % 16
    row = lax.broadcasted_iota(jnp.int32, (16, 128), 0)
    natural = (row % 8) * 2 + row // 8
    place = [(j % 2) * 8 + j // 2 for j in range(16)]
    left = [pltpu.roll(gram, (128 - place[j]) % 128, 1) if place[j] else gram for j in range(16)]
    right = [(row == place[j]).astype(F32) for j in range(16)]
    upper_all = jnp.zeros((16, 128), F32)
    inverse_all = jnp.zeros((16, 128), F32)
    for j in range(16):
        pivot = left[j][place[j]:place[j] + 1, :]
        root = lax.rsqrt(pivot)
        root = root * (1.5 - 0.5 * pivot * root * root)
        upper_row = left[j] * root
        inverse_row = right[j] * root
        for i in range(j + 1, 16):
            scale = upper_row[place[i]:place[i] + 1, :]
            left[i] = left[i] - scale * upper_row
            right[i] = right[i] - scale * inverse_row
        upper_row = jnp.where(natural >= j, upper_row, 0.0)
        if j:
            upper_row = pltpu.roll(upper_row, j, 1)
            inverse_row = pltpu.roll(inverse_row, j, 1)
        upper_all = jnp.where(lane == j, upper_row, upper_all)
        inverse_all = jnp.where(lane == j, inverse_row, inverse_all)

    upper[...] = jnp.zeros_like(upper)
    upper[pl.ds(0, 8, stride=2), :] = upper_all[0:8]
    upper[pl.ds(1, 8, stride=2), :] = upper_all[8:16]
    factors[...] = jnp.transpose(upper[...])[:, 0:16].reshape(8, 16, 16)
    factors_copy = pltpu.make_async_copy(factors, factors_hbm, sems.at[1])
    factors_copy.start()

    inverse_all = inverse_all * math.sqrt(points)
    row_freq = lax.broadcasted_iota(jnp.int32, (128, 128), 0) // 16
    lane_freq = lax.broadcasted_iota(jnp.int32, (128, 128), 1) // 16
    wide = jnp.where(row_freq == lane_freq, jnp.concatenate([inverse_all] * 8, axis=0), 0.0)
    w_high, w_middle, w_low = split3(jnp.transpose(wide))
    load.wait()
    high, middle, low = split3(columns[...])
    product = lax.dot_general(
        jnp.concatenate([w_high, w_high, w_middle, w_middle, w_high, w_low], axis=1),
        jnp.concatenate([high, middle, high, middle, low, high], axis=0),
        (((1,), (0,)), ((), ())),
        preferred_element_type=F32,
    )
    modes[...] = product.reshape(8, 16, 256)
    modes_copy = pltpu.make_async_copy(modes, modes_hbm, sems.at[2])
    modes_copy.start()
    factors_copy.wait()
    modes_copy.wait()


def fused(snapshots):
    points = snapshots.shape[1]
    dma = pltpu.SemaphoreType.DMA
    vmem = pltpu.VMEM
    columns, gram = pl.pallas_call(
        functools.partial(kernel, points),
        out_shape=(
            jax.ShapeDtypeStruct((128, 256), F32),
            jax.ShapeDtypeStruct((16, 128), F32),
        ),
        in_specs=[pl.BlockSpec(memory_space=pltpu.HBM)],
        out_specs=(pl.BlockSpec(memory_space=pl.ANY), pl.BlockSpec(memory_space=pltpu.VMEM)),
        scratch_shapes=[
            vmem((8, 64, 1024), F32),
            vmem((48, 192), BF16),
            vmem((8, 2, 2, 16, 256), F32),
            vmem((8, 2, 16, 256), F32),
            vmem((8, 16, 256), F32),
            vmem((8, 16, 256), F32),
            vmem((8, 2, 16, 128), F32),
            vmem((2, 128, 128), F32),
            vmem((128, 256), F32),
            vmem((16, 128), F32),
            vmem((8, 16, 128), F32),
            vmem((16, 128), F32),
            vmem((4, 16, 128), F32),
            dma((8,)),
            dma,
            dma((8,)),
            dma((8,)),
            dma((8,)),
            dma((8,)),
            dma((8,)),
            dma((8,)),
            dma((8,)),
            dma((8,)),
            dma((4,)),
            dma((4,)),
        ],
        compiler_params=pltpu.CompilerParams(
            collective_id=0, has_side_effects=True, vmem_limit_bytes=53 * 1024 * 1024
        ),
        name="welch_gram",
    )(snapshots)
    return pl.pallas_call(
        functools.partial(finish_kernel, points),
        out_shape=(
            jax.ShapeDtypeStruct((8, 16, 16), F32),
            jax.ShapeDtypeStruct((8, 16, 256), F32),
        ),
        in_specs=[pl.BlockSpec(memory_space=pltpu.VMEM), pl.BlockSpec(memory_space=pl.ANY)],
        out_specs=(pl.BlockSpec(memory_space=pl.ANY),) * 2,
        scratch_shapes=[
            vmem((128, 256), F32),
            vmem((128, 128), F32),
            vmem((8, 16, 16), F32),
            vmem((8, 16, 256), F32),
            dma((3,)),
        ],
        compiler_params=pltpu.CompilerParams(vmem_limit_bytes=16 * 1024 * 1024),
        name="factor_modes",
    )(gram, columns)


def local(snapshots):
    time_dev, points = snapshots.shape
    n_aa = lax.axis_size("aa")
    n_ba = lax.axis_size("ba")
    if (n_aa, n_ba, time_dev, points) == (8, 4, 64, 8192):
        return fused(snapshots)
    pts_dev = points // (n_aa * n_ba)
    block_len = time_dev * n_ba
    table = spectral_table(block_len, points)
    regrouped = lax.all_to_all(
        lax.all_to_all(snapshots, "aa", split_axis=1, concat_axis=0, tiled=True),
        "ba",
        split_axis=1,
        concat_axis=0,
        tiled=True,
    )
    arranged = regrouped.reshape(n_ba, n_aa, time_dev, pts_dev)
    table_parts = table.reshape(n_ba, time_dev, 2, FREQS)
    spectra = jnp.einsum("uasp,usgf->agfp", arranged, table_parts, precision=lax.Precision.HIGHEST)
    blocks = spectra.shape[0]
    columns = 2 * blocks
    product = jnp.einsum("bgfp,chfp->fbgch", spectra, spectra, precision=lax.Precision.HIGHEST)
    gram_sum = lax.psum(product.reshape(FREQS, columns, columns), ("aa", "ba"))
    lower_factor = jnp.linalg.cholesky(gram_sum)
    identity = jnp.broadcast_to(jnp.eye(columns, dtype=gram_sum.dtype), lower_factor.shape)
    inverse = lax.linalg.triangular_solve(lower_factor, identity, left_side=True, lower=True)
    pod_modes = math.sqrt(points) * jnp.einsum(
        "fibg,bgfp->fip",
        inverse.reshape(FREQS, columns, blocks, 2),
        spectra,
        precision=lax.Precision.HIGHEST,
    )
    return (jnp.swapaxes(lower_factor, 1, 2), pod_modes)


def solution(mesh):
    placed = (P(("aa", "ba"), None),)
    return jax.shard_map(
        local,
        mesh=mesh,
        in_specs=placed,
        out_specs=(P(), P(None, None, ("aa", "ba"))),
        check_vma=False,
    )
```

```python
import functools
import math

import jax
import jax.numpy as jnp
from jax import lax
from jax.experimental import pallas as pl
from jax.experimental.pallas import tpu as pltpu
from jax.sharding import PartitionSpec as P

FREQS = 8
MESH = pl.DeviceIdType.MESH
BF16 = jnp.bfloat16
F32 = jnp.float32

STEPS = ((2, 0), (2, 1), (1, 0), (1, 1), (3, 0), (3, 1), (0, 1), (0, 0))
GROUPS = ((0, 1, 2, 3), (4, 5, 6, 7))
STRAIGHT = (2, 3, 4, 5, 6)
REDUCED = (0, 1)


def spectral_table(block_len, points):
    sample = jnp.arange(block_len, dtype=jnp.int32)
    harmonic = jnp.arange(1, FREQS + 1, dtype=jnp.int32)
    phase_turns = (sample[:, None] * harmonic[None, :] % block_len).astype(jnp.float32) * (
        2.0 * math.pi / block_len
    )
    sample_angle = sample.astype(jnp.float32) * (2.0 * math.pi / block_len)
    window = 0.5 - 0.5 * jnp.cos(sample_angle)
    norm_scale = 1.0 / jnp.sqrt(points * jnp.sum(window * window))
    cosine = window[:, None] * jnp.cos(phase_turns) * norm_scale
    sine = -window[:, None] * jnp.sin(phase_turns) * norm_scale
    return jnp.stack([cosine, sine], axis=1)


def split_table(ba, points):
    row = lax.broadcasted_iota(jnp.int32, (16, 64), 0)
    sample = lax.broadcasted_iota(jnp.int32, (16, 64), 1) + ba * 64
    turns = (sample * (row // 2 + 1) + 64 * (row % 2)) % 256
    step = 2.0 * math.pi / 256
    window = 0.5 - 0.5 * jnp.cos(sample.astype(F32) * step)
    power = sum((0.5 - 0.5 * math.cos(n * step)) ** 2 for n in range(256))
    value = window * jnp.cos(turns.astype(F32) * step) * (1.0 / math.sqrt(points * power))
    rows = jnp.concatenate(split3(value), axis=0)
    return jnp.concatenate([rows] * 3, axis=1)


def split3(value):
    high = value.astype(BF16)
    rest = value - high.astype(F32)
    middle = rest.astype(BF16)
    low = (rest - middle.astype(F32)).astype(BF16)
    return high, middle, low


def kernel(
    points, x_hbm, columns_ref, gram_ref,
    x_buf, table, part, core_in, y_out, y_in, block_out, blocks,
    gram_out, gram_in, plane_out, plane_in,
    in_sem, core_send, core_recv, y_send, y_recv,
    block_send, block_recv, gram_send, gram_recv, plane_send, plane_recv,
):
    aa, ba = lax.axis_index("aa"), lax.axis_index("ba")
    z, x = aa // 2, aa % 2
    y, core = ba // 2, ba % 2
    other_core = 1 - core
    core_peer = (aa, y * 2 + other_core)
    y_peer = (aa, (1 - y) * 2 + core)
    owners = [((z + dz) % 4) * 2 + (x + dx) % 2 for dz, dx in STEPS]
    sources = [((z + 4 - dz) % 4) * 2 + (x + 2 - dx) % 2 for dz, dx in STEPS]
    plane = [(i // 4, i // 2 % 2, i % 2) for i in range(8)]
    plane_ids = [
        (z * 2 + (x + dx) % 2, ((y + dy) % 2) * 2 + (core + dc) % 2) for dx, dy, dc in plane
    ]
    line_ids = [(((z + dz) % 4) * 2 + x, ba) for dz in range(4)]

    barrier = pltpu.get_barrier_semaphore()
    peers = [(owner, ba) for owner in owners[:-1]]
    peers += [plane_ids[i] for i in range(1, 8) if plane[i] != (1, 0, 0)]
    peers += [(sources[k], (1 - y) * 2 + core) for k in STRAIGHT if STEPS[k][0]]
    for peer in peers:
        pl.semaphore_signal(barrier, inc=1, device_id=peer, device_id_type=MESH)
    loads = []
    for k in range(8):
        start = pl.multiple_of(owners[k] * 1024, 1024)
        load = pltpu.make_async_copy(x_hbm.at[:, pl.ds(start, 1024)], x_buf.at[k], in_sem.at[k])
        load.start()
        loads.append(load)
    table[...] = split_table(ba, points)

    sends = []

    def remote(src, dst, send, recv, device):
        copy = pltpu.make_async_remote_copy(
            src_ref=src, dst_ref=dst, send_sem=send, recv_sem=recv,
            device_id=device, device_id_type=MESH,
        )
        copy.start()
        sends.append(copy)
        return copy

    core_copies = []
    y_copies = {}

    def send_y(k, device):
        core_copies[k].wait_recv()
        y_out[k] = part[k, core, 1 - y] + core_in[k, 1 - y]
        y_copies[k] = remote(y_out.at[k], y_in.at[k], y_send.at[k], y_recv.at[k], device)

    pl.semaphore_wait(barrier, len(peers))
    for group in GROUPS:
        for tile in group:
            loads[tile].wait()
        terms = [jnp.concatenate(split3(x_buf[tile]), axis=0) for tile in group]
        rows = jnp.dot(table[...], jnp.concatenate(terms, axis=1), preferred_element_type=F32)
        total = rows[0:16] + rows[16:32] + rows[32:48]
        for n, tile in enumerate(group):
            for half in range(4):
                at = n * 1024 + half * 256
                part[tile, half % 2, half // 2] = total[:, at:at + 256]
        for tile in group:
            core_copies.append(
                remote(
                    part.at[tile, other_core], core_in.at[tile],
                    core_send.at[tile], core_recv.at[tile], core_peer,
                )
            )
    block_copies = []
    mine = pl.ds(pl.multiple_of(aa * 16, 16), 16)

    def send_block(k, total):
        block_out[k, 0] = total[:, 0:128]
        block_out[k, 1] = total[:, 128:256]
        block_copies.append(
            remote(
                block_out.at[k], blocks.at[:, mine, :],
                block_send.at[k], block_recv.at[k], (owners[k], ba),
            )
        )

    for k in REDUCED:
        send_y(k, y_peer)
    for k in STRAIGHT:
        send_y(k, (owners[k], (1 - y) * 2 + core))
        send_block(k, part[k, core, y] + core_in[k, y])
    send_y(7, y_peer)
    for k in REDUCED:
        y_copies[k].wait_recv()
        send_block(k, part[k, core, y] + core_in[k, y] + y_in[k])
    y_copies[7].wait_recv()
    total = part[7, core, y] + core_in[7, y] + y_in[7]
    blocks[0, mine, :] = total[:, 0:128]
    blocks[1, mine, :] = total[:, 128:256]
    for copy in block_copies:
        copy.wait_recv()
    for k in STRAIGHT:
        y_copies[k].wait_recv()
        theirs = pl.ds(pl.multiple_of(sources[k] * 16, 16), 16)
        blocks[0, theirs, :] += y_in[k, :, 0:128]
        blocks[1, theirs, :] += y_in[k, :, 128:256]

    columns = jnp.concatenate(
        [
            jnp.concatenate([blocks[half, pl.ds(r, 8, stride=16), :] for r in range(16)], axis=0)
            for half in range(2)
        ],
        axis=1,
    )
    columns_ref[...] = columns
    high, middle, low = split3(columns)
    contract_last = (((1,), (1,)), ((), ()))
    product = lax.dot_general(
        jnp.concatenate([high, middle, low], axis=0),
        jnp.concatenate([high, middle], axis=0),
        contract_last,
        preferred_element_type=F32,
    )
    high_low = lax.dot_general(high, low, contract_last, preferred_element_type=F32)
    gram_full = (product[0:128, 0:128] + product[128:256, 128:256]) + (
        (product[0:128, 128:256] + product[128:256, 0:128]) + (product[256:384, 0:128] + high_low)
    )
    row_freq = lax.broadcasted_iota(jnp.int32, (128, 128), 0) // 16
    lane_freq = lax.broadcasted_iota(jnp.int32, (128, 128), 1) // 16
    same = row_freq == lane_freq
    kept = jnp.where(same, gram_full, 0.0).reshape(8, 16, 128)
    gram_out[...] = ((kept[0] + kept[1]) + (kept[2] + kept[3])) + ((kept[4] + kept[5]) + (kept[6] + kept[7]))

    copies = [
        remote(gram_out, gram_in.at[i], gram_send.at[i], gram_recv.at[i], plane_ids[i]) for i in range(1, 8)
    ]
    for copy in sends[:-7]:
        copy.wait_send()
    for copy in copies:
        copy.wait_recv()
    pairs = [gram_out[...] + gram_in[1]] + [gram_in[i] + gram_in[i + 1] for i in (2, 4, 6)]
    plane_out[...] = (pairs[0] + pairs[1]) + (pairs[2] + pairs[3])
    copies = [
        remote(plane_out, plane_in.at[i], plane_send.at[i], plane_recv.at[i], line_ids[i]) for i in range(1, 4)
    ]
    for copy in sends[-10:-3]:
        copy.wait_send()
    for copy in copies:
        copy.wait_recv()
    gram_ref[...] = (plane_out[...] + plane_in[2]) + (plane_in[1] + plane_in[3])
    for copy in sends[-3:]:
        copy.wait_send()


def finish_kernel(points, gram_ref, columns_ref, factors_hbm, modes_hbm, upper, factors, modes, sems):
    high, middle, low = split3(columns_ref[...])
    gram = gram_ref[...]
    lane = lax.broadcasted_iota(jnp.int32, (16, 128), 1) % 16
    row = lax.broadcasted_iota(jnp.int32, (16, 128), 0)
    natural = (row % 8) * 2 + row // 8
    place = [(j % 2) * 8 + j // 2 for j in range(16)]
    left = [pltpu.roll(gram, (128 - place[j]) % 128, 1) if place[j] else gram for j in range(16)]
    right = [(row == place[j]).astype(F32) for j in range(16)]
    upper_all = jnp.zeros((16, 128), F32)
    inverse_all = jnp.zeros((16, 128), F32)
    for j in range(16):
        pivot = left[j][place[j]:place[j] + 1, :]
        root = lax.rsqrt(pivot)
        root = root * (1.5 - 0.5 * pivot * root * root)
        upper_row = left[j] * root
        inverse_row = right[j] * root
        for i in range(j + 1, 16):
            scale = upper_row[place[i]:place[i] + 1, :]
            left[i] = left[i] - scale * upper_row
            right[i] = right[i] - scale * inverse_row
        upper_row = jnp.where(natural >= j, upper_row, 0.0)
        if j:
            upper_row = pltpu.roll(upper_row, j, 1)
            inverse_row = pltpu.roll(inverse_row, j, 1)
        upper_all = jnp.where(lane == j, upper_row, upper_all)
        inverse_all = jnp.where(lane == j, inverse_row, inverse_all)

    upper[...] = jnp.zeros_like(upper)
    upper[pl.ds(0, 8, stride=2), :] = upper_all[0:8]
    upper[pl.ds(1, 8, stride=2), :] = upper_all[8:16]
    factors[...] = jnp.transpose(upper[...])[:, 0:16].reshape(8, 16, 16)
    factors_copy = pltpu.make_async_copy(factors, factors_hbm, sems.at[0])
    factors_copy.start()

    inverse_all = inverse_all * math.sqrt(points)
    row_freq = lax.broadcasted_iota(jnp.int32, (128, 128), 0) // 16
    lane_freq = lax.broadcasted_iota(jnp.int32, (128, 128), 1) // 16
    wide = jnp.where(row_freq == lane_freq, jnp.concatenate([inverse_all] * 8, axis=0), 0.0)
    w_high, w_middle, w_low = split3(jnp.transpose(wide))
    product = lax.dot_general(
        jnp.concatenate([w_high, w_high, w_middle, w_middle, w_high, w_low], axis=1),
        jnp.concatenate([high, middle, high, middle, low, high], axis=0),
        (((1,), (0,)), ((), ())),
        preferred_element_type=F32,
    )
    modes[...] = product.reshape(8, 16, 256)
    modes_copy = pltpu.make_async_copy(modes, modes_hbm, sems.at[1])
    modes_copy.start()
    factors_copy.wait()
    modes_copy.wait()


def fused(snapshots):
    points = snapshots.shape[1]
    dma = pltpu.SemaphoreType.DMA
    vmem = pltpu.VMEM
    columns, gram = pl.pallas_call(
        functools.partial(kernel, points),
        out_shape=(
            jax.ShapeDtypeStruct((128, 256), F32),
            jax.ShapeDtypeStruct((16, 128), F32),
        ),
        in_specs=[pl.BlockSpec(memory_space=pltpu.HBM)],
        out_specs=(pl.BlockSpec(memory_space=pltpu.VMEM),) * 2,
        scratch_shapes=[
            vmem((8, 64, 1024), F32),
            vmem((48, 192), BF16),
            vmem((8, 2, 2, 16, 256), F32),
            vmem((8, 2, 16, 256), F32),
            vmem((8, 16, 256), F32),
            vmem((8, 16, 256), F32),
            vmem((8, 2, 16, 128), F32),
            vmem((2, 128, 128), F32),
            vmem((16, 128), F32),
            vmem((8, 16, 128), F32),
            vmem((16, 128), F32),
            vmem((4, 16, 128), F32),
            dma((8,)),
            dma((8,)),
            dma((8,)),
            dma((8,)),
            dma((8,)),
            dma((8,)),
            dma((8,)),
            dma((8,)),
            dma((8,)),
            dma((4,)),
            dma((4,)),
        ],
        compiler_params=pltpu.CompilerParams(
            collective_id=0, has_side_effects=True, vmem_limit_bytes=53 * 1024 * 1024
        ),
        name="welch_gram",
    )(snapshots)
    return pl.pallas_call(
        functools.partial(finish_kernel, points),
        out_shape=(
            jax.ShapeDtypeStruct((8, 16, 16), F32),
            jax.ShapeDtypeStruct((8, 16, 256), F32),
        ),
        in_specs=[pl.BlockSpec(memory_space=pltpu.VMEM)] * 2,
        out_specs=(pl.BlockSpec(memory_space=pl.ANY),) * 2,
        scratch_shapes=[
            vmem((128, 128), F32),
            vmem((8, 16, 16), F32),
            vmem((8, 16, 256), F32),
            dma((2,)),
        ],
        compiler_params=pltpu.CompilerParams(vmem_limit_bytes=16 * 1024 * 1024),
        name="factor_modes",
    )(gram, columns)


def local(snapshots):
    time_dev, points = snapshots.shape
    n_aa = lax.axis_size("aa")
    n_ba = lax.axis_size("ba")
    if (n_aa, n_ba, time_dev, points) == (8, 4, 64, 8192):
        return fused(snapshots)
    pts_dev = points // (n_aa * n_ba)
    block_len = time_dev * n_ba
    table = spectral_table(block_len, points)
    regrouped = lax.all_to_all(
        lax.all_to_all(snapshots, "aa", split_axis=1, concat_axis=0, tiled=True),
        "ba",
        split_axis=1,
        concat_axis=0,
        tiled=True,
    )
    arranged = regrouped.reshape(n_ba, n_aa, time_dev, pts_dev)
    table_parts = table.reshape(n_ba, time_dev, 2, FREQS)
    spectra = jnp.einsum("uasp,usgf->agfp", arranged, table_parts, precision=lax.Precision.HIGHEST)
    blocks = spectra.shape[0]
    columns = 2 * blocks
    product = jnp.einsum("bgfp,chfp->fbgch", spectra, spectra, precision=lax.Precision.HIGHEST)
    gram_sum = lax.psum(product.reshape(FREQS, columns, columns), ("aa", "ba"))
    lower_factor = jnp.linalg.cholesky(gram_sum)
    identity = jnp.broadcast_to(jnp.eye(columns, dtype=gram_sum.dtype), lower_factor.shape)
    inverse = lax.linalg.triangular_solve(lower_factor, identity, left_side=True, lower=True)
    pod_modes = math.sqrt(points) * jnp.einsum(
        "fibg,bgfp->fip",
        inverse.reshape(FREQS, columns, blocks, 2),
        spectra,
        precision=lax.Precision.HIGHEST,
    )
    return (jnp.swapaxes(lower_factor, 1, 2), pod_modes)


def solution(mesh):
    placed = (P(("aa", "ba"), None),)
    return jax.shard_map(
        local,
        mesh=mesh,
        in_specs=placed,
        out_specs=(P(), P(None, None, ("aa", "ba"))),
        check_vma=False,
    )
```

```python
import functools
import math

import jax
import jax.numpy as jnp
from jax import lax
from jax.experimental import pallas as pl
from jax.experimental.pallas import tpu as pltpu
from jax.sharding import PartitionSpec as P

FREQS = 8
MESH = pl.DeviceIdType.MESH
BF16 = jnp.bfloat16
F32 = jnp.float32

STEPS = ((2, 0), (2, 1), (1, 0), (1, 1), (3, 0), (3, 1), (0, 1), (0, 0))
GROUPS = ((0, 1, 2, 3), (4, 5, 6, 7))
STRAIGHT = (4, 5, 6)
REDUCED = (0, 1, 2, 3)


def spectral_table(block_len, points):
    sample = jnp.arange(block_len, dtype=jnp.int32)
    harmonic = jnp.arange(1, FREQS + 1, dtype=jnp.int32)
    phase_turns = (sample[:, None] * harmonic[None, :] % block_len).astype(jnp.float32) * (
        2.0 * math.pi / block_len
    )
    sample_angle = sample.astype(jnp.float32) * (2.0 * math.pi / block_len)
    window = 0.5 - 0.5 * jnp.cos(sample_angle)
    norm_scale = 1.0 / jnp.sqrt(points * jnp.sum(window * window))
    cosine = window[:, None] * jnp.cos(phase_turns) * norm_scale
    sine = -window[:, None] * jnp.sin(phase_turns) * norm_scale
    return jnp.stack([cosine, sine], axis=1)


def split_table(ba, points):
    row = lax.broadcasted_iota(jnp.int32, (16, 64), 0)
    sample = lax.broadcasted_iota(jnp.int32, (16, 64), 1) + ba * 64
    turns = (sample * (row // 2 + 1) + 64 * (row % 2)) % 256
    step = 2.0 * math.pi / 256
    window = 0.5 - 0.5 * jnp.cos(sample.astype(F32) * step)
    power = sum((0.5 - 0.5 * math.cos(n * step)) ** 2 for n in range(256))
    value = window * jnp.cos(turns.astype(F32) * step) * (1.0 / math.sqrt(points * power))
    rows = jnp.concatenate(split3(value), axis=0)
    return jnp.concatenate([rows] * 3, axis=1)


def split3(value):
    high = value.astype(BF16)
    rest = value - high.astype(F32)
    middle = rest.astype(BF16)
    low = (rest - middle.astype(F32)).astype(BF16)
    return high, middle, low


def kernel(
    points, x_hbm, columns_ref, gram_ref,
    x_buf, table, part, core_in, y_out, y_in, block_out, blocks,
    gram_out, gram_in, plane_out, plane_in,
    in_sem, core_send, core_recv, y_send, y_recv,
    block_send, block_recv, gram_send, gram_recv, plane_send, plane_recv,
):
    aa, ba = lax.axis_index("aa"), lax.axis_index("ba")
    z, x = aa // 2, aa % 2
    y, core = ba // 2, ba % 2
    other_core = 1 - core
    core_peer = (aa, y * 2 + other_core)
    y_peer = (aa, (1 - y) * 2 + core)
    owners = [((z + dz) % 4) * 2 + (x + dx) % 2 for dz, dx in STEPS]
    sources = [((z + 4 - dz) % 4) * 2 + (x + 2 - dx) % 2 for dz, dx in STEPS]
    plane = [(i // 4, i // 2 % 2, i % 2) for i in range(8)]
    plane_ids = [
        (z * 2 + (x + dx) % 2, ((y + dy) % 2) * 2 + (core + dc) % 2) for dx, dy, dc in plane
    ]
    line_ids = [(((z + dz) % 4) * 2 + x, ba) for dz in range(4)]

    barrier = pltpu.get_barrier_semaphore()
    peers = [(owner, ba) for owner in owners[:-1]]
    peers += [plane_ids[i] for i in range(1, 8) if plane[i] != (1, 0, 0)]
    peers += [(sources[k], (1 - y) * 2 + core) for k in STRAIGHT if STEPS[k][0]]
    for peer in peers:
        pl.semaphore_signal(barrier, inc=1, device_id=peer, device_id_type=MESH)
    loads = []
    for k in range(8):
        start = pl.multiple_of(owners[k] * 1024, 1024)
        load = pltpu.make_async_copy(x_hbm.at[:, pl.ds(start, 1024)], x_buf.at[k], in_sem.at[k])
        load.start()
        loads.append(load)
    table[...] = split_table(ba, points)

    sends = []

    def remote(src, dst, send, recv, device):
        copy = pltpu.make_async_remote_copy(
            src_ref=src, dst_ref=dst, send_sem=send, recv_sem=recv,
            device_id=device, device_id_type=MESH,
        )
        copy.start()
        sends.append(copy)
        return copy

    core_copies = []
    y_copies = {}

    def send_y(k, device):
        core_copies[k].wait_recv()
        y_out[k] = part[k, core, 1 - y] + core_in[k, 1 - y]
        y_copies[k] = remote(y_out.at[k], y_in.at[k], y_send.at[k], y_recv.at[k], device)

    pl.semaphore_wait(barrier, len(peers))
    for group in GROUPS:
        for tile in group:
            loads[tile].wait()
        terms = [jnp.concatenate(split3(x_buf[tile]), axis=0) for tile in group]
        rows = jnp.dot(table[...], jnp.concatenate(terms, axis=1), preferred_element_type=F32)
        total = rows[0:16] + rows[16:32] + rows[32:48]
        for n, tile in enumerate(group):
            for half in range(4):
                at = n * 1024 + half * 256
                part[tile, half % 2, half // 2] = total[:, at:at + 256]
        for tile in group:
            core_copies.append(
                remote(
                    part.at[tile, other_core], core_in.at[tile],
                    core_send.at[tile], core_recv.at[tile], core_peer,
                )
            )
    block_copies = []
    mine = pl.ds(pl.multiple_of(aa * 16, 16), 16)

    def send_block(k, total):
        block_out[k, 0] = total[:, 0:128]
        block_out[k, 1] = total[:, 128:256]
        block_copies.append(
            remote(
                block_out.at[k], blocks.at[:, mine, :],
                block_send.at[k], block_recv.at[k], (owners[k], ba),
            )
        )

    for k in REDUCED:
        send_y(k, y_peer)
    for k in STRAIGHT:
        send_y(k, (owners[k], (1 - y) * 2 + core))
        send_block(k, part[k, core, y] + core_in[k, y])
    send_y(7, y_peer)
    for k in REDUCED:
        y_copies[k].wait_recv()
        send_block(k, part[k, core, y] + core_in[k, y] + y_in[k])
    y_copies[7].wait_recv()
    total = part[7, core, y] + core_in[7, y] + y_in[7]
    blocks[0, mine, :] = total[:, 0:128]
    blocks[1, mine, :] = total[:, 128:256]
    for copy in block_copies:
        copy.wait_recv()
    for k in STRAIGHT:
        y_copies[k].wait_recv()
        theirs = pl.ds(pl.multiple_of(sources[k] * 16, 16), 16)
        blocks[0, theirs, :] += y_in[k, :, 0:128]
        blocks[1, theirs, :] += y_in[k, :, 128:256]

    columns = jnp.concatenate(
        [
            jnp.concatenate([blocks[half, pl.ds(r, 8, stride=16), :] for r in range(16)], axis=0)
            for half in range(2)
        ],
        axis=1,
    )
    columns_ref[...] = columns
    high, middle, low = split3(columns)
    contract_last = (((1,), (1,)), ((), ()))
    product = lax.dot_general(
        jnp.concatenate([high, middle, low], axis=0),
        jnp.concatenate([high, middle], axis=0),
        contract_last,
        preferred_element_type=F32,
    )
    high_low = lax.dot_general(high, low, contract_last, preferred_element_type=F32)
    gram_full = (product[0:128, 0:128] + product[128:256, 128:256]) + (
        (product[0:128, 128:256] + product[128:256, 0:128]) + (product[256:384, 0:128] + high_low)
    )
    row_freq = lax.broadcasted_iota(jnp.int32, (128, 128), 0) // 16
    lane_freq = lax.broadcasted_iota(jnp.int32, (128, 128), 1) // 16
    same = row_freq == lane_freq
    kept = jnp.where(same, gram_full, 0.0).reshape(8, 16, 128)
    gram_out[...] = ((kept[0] + kept[1]) + (kept[2] + kept[3])) + ((kept[4] + kept[5]) + (kept[6] + kept[7]))

    copies = [
        remote(gram_out, gram_in.at[i], gram_send.at[i], gram_recv.at[i], plane_ids[i]) for i in range(1, 8)
    ]
    for copy in sends[:-7]:
        copy.wait_send()
    for copy in copies:
        copy.wait_recv()
    pairs = [gram_out[...] + gram_in[1]] + [gram_in[i] + gram_in[i + 1] for i in (2, 4, 6)]
    plane_out[...] = (pairs[0] + pairs[1]) + (pairs[2] + pairs[3])
    copies = [
        remote(plane_out, plane_in.at[i], plane_send.at[i], plane_recv.at[i], line_ids[i]) for i in range(1, 4)
    ]
    for copy in sends[-10:-3]:
        copy.wait_send()
    for copy in copies:
        copy.wait_recv()
    gram_ref[...] = (plane_out[...] + plane_in[2]) + (plane_in[1] + plane_in[3])
    for copy in sends[-3:]:
        copy.wait_send()


def finish_kernel(points, gram_ref, columns_ref, factors_hbm, modes_hbm, upper, factors, modes, sems):
    high, middle, low = split3(columns_ref[...])
    gram = gram_ref[...]
    lane = lax.broadcasted_iota(jnp.int32, (16, 128), 1) % 16
    row = lax.broadcasted_iota(jnp.int32, (16, 128), 0)
    natural = (row % 8) * 2 + row // 8
    place = [(j % 2) * 8 + j // 2 for j in range(16)]
    left = [pltpu.roll(gram, (128 - place[j]) % 128, 1) if place[j] else gram for j in range(16)]
    right = [(row == place[j]).astype(F32) for j in range(16)]
    upper_all = jnp.zeros((16, 128), F32)
    inverse_all = jnp.zeros((16, 128), F32)
    for j in range(16):
        pivot = left[j][place[j]:place[j] + 1, :]
        root = lax.rsqrt(pivot)
        root = root * (1.5 - 0.5 * pivot * root * root)
        upper_row = left[j] * root
        inverse_row = right[j] * root
        for i in range(j + 1, 16):
            scale = upper_row[place[i]:place[i] + 1, :]
            left[i] = left[i] - scale * upper_row
            right[i] = right[i] - scale * inverse_row
        upper_row = jnp.where(natural >= j, upper_row, 0.0)
        if j:
            upper_row = pltpu.roll(upper_row, j, 1)
            inverse_row = pltpu.roll(inverse_row, j, 1)
        upper_all = jnp.where(lane == j, upper_row, upper_all)
        inverse_all = jnp.where(lane == j, inverse_row, inverse_all)

    upper[...] = jnp.zeros_like(upper)
    upper[pl.ds(0, 8, stride=2), :] = upper_all[0:8]
    upper[pl.ds(1, 8, stride=2), :] = upper_all[8:16]
    factors[...] = jnp.transpose(upper[...])[:, 0:16].reshape(8, 16, 16)
    factors_copy = pltpu.make_async_copy(factors, factors_hbm, sems.at[0])
    factors_copy.start()

    inverse_all = inverse_all * math.sqrt(points)
    row_freq = lax.broadcasted_iota(jnp.int32, (128, 128), 0) // 16
    lane_freq = lax.broadcasted_iota(jnp.int32, (128, 128), 1) // 16
    wide = jnp.where(row_freq == lane_freq, jnp.concatenate([inverse_all] * 8, axis=0), 0.0)
    w_high, w_middle, w_low = split3(jnp.transpose(wide))
    product = lax.dot_general(
        jnp.concatenate([w_high, w_high, w_middle, w_middle, w_high, w_low], axis=1),
        jnp.concatenate([high, middle, high, middle, low, high], axis=0),
        (((1,), (0,)), ((), ())),
        preferred_element_type=F32,
    )
    modes[...] = product.reshape(8, 16, 256)
    modes_copy = pltpu.make_async_copy(modes, modes_hbm, sems.at[1])
    modes_copy.start()
    factors_copy.wait()
    modes_copy.wait()


def fused(snapshots):
    points = snapshots.shape[1]
    dma = pltpu.SemaphoreType.DMA
    vmem = pltpu.VMEM
    columns, gram = pl.pallas_call(
        functools.partial(kernel, points),
        out_shape=(
            jax.ShapeDtypeStruct((128, 256), F32),
            jax.ShapeDtypeStruct((16, 128), F32),
        ),
        in_specs=[pl.BlockSpec(memory_space=pltpu.HBM)],
        out_specs=(pl.BlockSpec(memory_space=pltpu.VMEM),) * 2,
        scratch_shapes=[
            vmem((8, 64, 1024), F32),
            vmem((48, 192), BF16),
            vmem((8, 2, 2, 16, 256), F32),
            vmem((8, 2, 16, 256), F32),
            vmem((8, 16, 256), F32),
            vmem((8, 16, 256), F32),
            vmem((8, 2, 16, 128), F32),
            vmem((2, 128, 128), F32),
            vmem((16, 128), F32),
            vmem((8, 16, 128), F32),
            vmem((16, 128), F32),
            vmem((4, 16, 128), F32),
            dma((8,)),
            dma((8,)),
            dma((8,)),
            dma((8,)),
            dma((8,)),
            dma((8,)),
            dma((8,)),
            dma((8,)),
            dma((8,)),
            dma((4,)),
            dma((4,)),
        ],
        compiler_params=pltpu.CompilerParams(
            collective_id=0, has_side_effects=True, vmem_limit_bytes=53 * 1024 * 1024
        ),
        name="welch_gram",
    )(snapshots)
    return pl.pallas_call(
        functools.partial(finish_kernel, points),
        out_shape=(
            jax.ShapeDtypeStruct((8, 16, 16), F32),
            jax.ShapeDtypeStruct((8, 16, 256), F32),
        ),
        in_specs=[pl.BlockSpec(memory_space=pltpu.VMEM)] * 2,
        out_specs=(pl.BlockSpec(memory_space=pl.ANY),) * 2,
        scratch_shapes=[
            vmem((128, 128), F32),
            vmem((8, 16, 16), F32),
            vmem((8, 16, 256), F32),
            dma((2,)),
        ],
        compiler_params=pltpu.CompilerParams(vmem_limit_bytes=16 * 1024 * 1024),
        name="factor_modes",
    )(gram, columns)


def local(snapshots):
    time_dev, points = snapshots.shape
    n_aa = lax.axis_size("aa")
    n_ba = lax.axis_size("ba")
    if (n_aa, n_ba, time_dev, points) == (8, 4, 64, 8192):
        return fused(snapshots)
    pts_dev = points // (n_aa * n_ba)
    block_len = time_dev * n_ba
    table = spectral_table(block_len, points)
    regrouped = lax.all_to_all(
        lax.all_to_all(snapshots, "aa", split_axis=1, concat_axis=0, tiled=True),
        "ba",
        split_axis=1,
        concat_axis=0,
        tiled=True,
    )
    arranged = regrouped.reshape(n_ba, n_aa, time_dev, pts_dev)
    table_parts = table.reshape(n_ba, time_dev, 2, FREQS)
    spectra = jnp.einsum("uasp,usgf->agfp", arranged, table_parts, precision=lax.Precision.HIGHEST)
    blocks = spectra.shape[0]
    columns = 2 * blocks
    product = jnp.einsum("bgfp,chfp->fbgch", spectra, spectra, precision=lax.Precision.HIGHEST)
    gram_sum = lax.psum(product.reshape(FREQS, columns, columns), ("aa", "ba"))
    lower_factor = jnp.linalg.cholesky(gram_sum)
    identity = jnp.broadcast_to(jnp.eye(columns, dtype=gram_sum.dtype), lower_factor.shape)
    inverse = lax.linalg.triangular_solve(lower_factor, identity, left_side=True, lower=True)
    pod_modes = math.sqrt(points) * jnp.einsum(
        "fibg,bgfp->fip",
        inverse.reshape(FREQS, columns, blocks, 2),
        spectra,
        precision=lax.Precision.HIGHEST,
    )
    return (jnp.swapaxes(lower_factor, 1, 2), pod_modes)


def solution(mesh):
    placed = (P(("aa", "ba"), None),)
    return jax.shard_map(
        local,
        mesh=mesh,
        in_specs=placed,
        out_specs=(P(), P(None, None, ("aa", "ba"))),
        check_vma=False,
    )
```

```python
import functools
import math

import jax
import jax.numpy as jnp
from jax import lax
from jax.experimental import pallas as pl
from jax.experimental.pallas import tpu as pltpu
from jax.sharding import PartitionSpec as P

FREQS = 8
MESH = pl.DeviceIdType.MESH
BF16 = jnp.bfloat16
F32 = jnp.float32

STEPS = ((2, 0), (2, 1), (1, 0), (1, 1), (3, 0), (3, 1), (0, 1), (0, 0))
GROUPS = ((0, 1), (2, 3, 4), (5, 6, 7))
STRAIGHT = (4, 5, 6)
REDUCED = (0, 1, 2, 3)


def spectral_table(block_len, points):
    sample = jnp.arange(block_len, dtype=jnp.int32)
    harmonic = jnp.arange(1, FREQS + 1, dtype=jnp.int32)
    phase_turns = (sample[:, None] * harmonic[None, :] % block_len).astype(jnp.float32) * (
        2.0 * math.pi / block_len
    )
    sample_angle = sample.astype(jnp.float32) * (2.0 * math.pi / block_len)
    window = 0.5 - 0.5 * jnp.cos(sample_angle)
    norm_scale = 1.0 / jnp.sqrt(points * jnp.sum(window * window))
    cosine = window[:, None] * jnp.cos(phase_turns) * norm_scale
    sine = -window[:, None] * jnp.sin(phase_turns) * norm_scale
    return jnp.stack([cosine, sine], axis=1)


def split_table(ba, points):
    row = lax.broadcasted_iota(jnp.int32, (16, 64), 0)
    sample = lax.broadcasted_iota(jnp.int32, (16, 64), 1) + ba * 64
    turns = (sample * (row // 2 + 1) + 64 * (row % 2)) % 256
    step = 2.0 * math.pi / 256
    window = 0.5 - 0.5 * jnp.cos(sample.astype(F32) * step)
    power = sum((0.5 - 0.5 * math.cos(n * step)) ** 2 for n in range(256))
    value = window * jnp.cos(turns.astype(F32) * step) * (1.0 / math.sqrt(points * power))
    rows = jnp.concatenate(split3(value), axis=0)
    return jnp.concatenate([rows] * 3, axis=1)


def split3(value):
    high = value.astype(BF16)
    rest = value - high.astype(F32)
    middle = rest.astype(BF16)
    low = (rest - middle.astype(F32)).astype(BF16)
    return high, middle, low


def kernel(
    points, x_hbm, columns_ref, gram_ref,
    x_buf, table, part, core_in, y_out, y_in, block_out, blocks,
    gram_out, gram_in, plane_out, plane_in,
    in_sem, core_send, core_recv, y_send, y_recv,
    block_send, block_recv, gram_send, gram_recv, plane_send, plane_recv,
):
    aa, ba = lax.axis_index("aa"), lax.axis_index("ba")
    z, x = aa // 2, aa % 2
    y, core = ba // 2, ba % 2
    other_core = 1 - core
    core_peer = (aa, y * 2 + other_core)
    y_peer = (aa, (1 - y) * 2 + core)
    owners = [((z + dz) % 4) * 2 + (x + dx) % 2 for dz, dx in STEPS]
    sources = [((z + 4 - dz) % 4) * 2 + (x + 2 - dx) % 2 for dz, dx in STEPS]
    plane = [(i // 4, i // 2 % 2, i % 2) for i in range(8)]
    plane_ids = [
        (z * 2 + (x + dx) % 2, ((y + dy) % 2) * 2 + (core + dc) % 2) for dx, dy, dc in plane
    ]
    line_ids = [(((z + dz) % 4) * 2 + x, ba) for dz in range(4)]

    barrier = pltpu.get_barrier_semaphore()
    peers = [(owner, ba) for owner in owners[:-1]]
    peers += [plane_ids[i] for i in range(1, 8) if plane[i] != (1, 0, 0)]
    peers += [(sources[k], (1 - y) * 2 + core) for k in STRAIGHT if STEPS[k][0]]
    for peer in peers:
        pl.semaphore_signal(barrier, inc=1, device_id=peer, device_id_type=MESH)
    loads = []
    for k in range(8):
        start = pl.multiple_of(owners[k] * 1024, 1024)
        load = pltpu.make_async_copy(x_hbm.at[:, pl.ds(start, 1024)], x_buf.at[k], in_sem.at[k])
        load.start()
        loads.append(load)
    table[...] = split_table(ba, points)

    sends = []

    def remote(src, dst, send, recv, device):
        copy = pltpu.make_async_remote_copy(
            src_ref=src, dst_ref=dst, send_sem=send, recv_sem=recv,
            device_id=device, device_id_type=MESH,
        )
        copy.start()
        sends.append(copy)
        return copy

    core_copies = []
    y_copies = {}

    def send_y(k, device):
        core_copies[k].wait_recv()
        y_out[k] = part[k, core, 1 - y] + core_in[k, 1 - y]
        y_copies[k] = remote(y_out.at[k], y_in.at[k], y_send.at[k], y_recv.at[k], device)

    pl.semaphore_wait(barrier, len(peers))
    for group in GROUPS:
        for tile in group:
            loads[tile].wait()
        terms = [jnp.concatenate(split3(x_buf[tile]), axis=0) for tile in group]
        rows = jnp.dot(table[...], jnp.concatenate(terms, axis=1), preferred_element_type=F32)
        total = rows[0:16] + rows[16:32] + rows[32:48]
        for n, tile in enumerate(group):
            for half in range(4):
                at = n * 1024 + half * 256
                part[tile, half % 2, half // 2] = total[:, at:at + 256]
        for tile in group:
            core_copies.append(
                remote(
                    part.at[tile, other_core], core_in.at[tile],
                    core_send.at[tile], core_recv.at[tile], core_peer,
                )
            )
    block_copies = []
    mine = pl.ds(pl.multiple_of(aa * 16, 16), 16)

    def send_block(k, total):
        block_out[k, 0] = total[:, 0:128]
        block_out[k, 1] = total[:, 128:256]
        block_copies.append(
            remote(
                block_out.at[k], blocks.at[:, mine, :],
                block_send.at[k], block_recv.at[k], (owners[k], ba),
            )
        )

    for k in REDUCED:
        send_y(k, y_peer)
    for k in STRAIGHT:
        send_y(k, (owners[k], (1 - y) * 2 + core))
        send_block(k, part[k, core, y] + core_in[k, y])
    send_y(7, y_peer)
    for k in REDUCED:
        y_copies[k].wait_recv()
        send_block(k, part[k, core, y] + core_in[k, y] + y_in[k])
    y_copies[7].wait_recv()
    total = part[7, core, y] + core_in[7, y] + y_in[7]
    blocks[0, mine, :] = total[:, 0:128]
    blocks[1, mine, :] = total[:, 128:256]
    for copy in block_copies:
        copy.wait_recv()
    for k in STRAIGHT:
        y_copies[k].wait_recv()
        theirs = pl.ds(pl.multiple_of(sources[k] * 16, 16), 16)
        blocks[0, theirs, :] += y_in[k, :, 0:128]
        blocks[1, theirs, :] += y_in[k, :, 128:256]

    columns = jnp.concatenate(
        [
            jnp.concatenate([blocks[half, pl.ds(r, 8, stride=16), :] for r in range(16)], axis=0)
            for half in range(2)
        ],
        axis=1,
    )
    columns_ref[...] = columns
    high, middle, low = split3(columns)
    contract_last = (((1,), (1,)), ((), ()))
    product = lax.dot_general(
        jnp.concatenate([high, middle, low], axis=0),
        jnp.concatenate([high, middle], axis=0),
        contract_last,
        preferred_element_type=F32,
    )
    high_low = lax.dot_general(high, low, contract_last, preferred_element_type=F32)
    gram_full = (product[0:128, 0:128] + product[128:256, 128:256]) + (
        (product[0:128, 128:256] + product[128:256, 0:128]) + (product[256:384, 0:128] + high_low)
    )
    row_freq = lax.broadcasted_iota(jnp.int32, (128, 128), 0) // 16
    lane_freq = lax.broadcasted_iota(jnp.int32, (128, 128), 1) // 16
    same = row_freq == lane_freq
    kept = jnp.where(same, gram_full, 0.0).reshape(8, 16, 128)
    gram_out[...] = ((kept[0] + kept[1]) + (kept[2] + kept[3])) + ((kept[4] + kept[5]) + (kept[6] + kept[7]))

    copies = [
        remote(gram_out, gram_in.at[i], gram_send.at[i], gram_recv.at[i], plane_ids[i]) for i in range(1, 8)
    ]
    for copy in sends[:-7]:
        copy.wait_send()
    for copy in copies:
        copy.wait_recv()
    pairs = [gram_out[...] + gram_in[1]] + [gram_in[i] + gram_in[i + 1] for i in (2, 4, 6)]
    plane_out[...] = (pairs[0] + pairs[1]) + (pairs[2] + pairs[3])
    copies = [
        remote(plane_out, plane_in.at[i], plane_send.at[i], plane_recv.at[i], line_ids[i]) for i in range(1, 4)
    ]
    for copy in sends[-10:-3]:
        copy.wait_send()
    for copy in copies:
        copy.wait_recv()
    gram_ref[...] = (plane_out[...] + plane_in[2]) + (plane_in[1] + plane_in[3])
    for copy in sends[-3:]:
        copy.wait_send()


def finish_kernel(points, gram_ref, columns_ref, factors_hbm, modes_hbm, upper, factors, modes, sems):
    high, middle, low = split3(columns_ref[...])
    gram = gram_ref[...]
    lane = lax.broadcasted_iota(jnp.int32, (16, 128), 1) % 16
    row = lax.broadcasted_iota(jnp.int32, (16, 128), 0)
    natural = (row % 8) * 2 + row // 8
    place = [(j % 2) * 8 + j // 2 for j in range(16)]
    left = [pltpu.roll(gram, (128 - place[j]) % 128, 1) if place[j] else gram for j in range(16)]
    right = [(row == place[j]).astype(F32) for j in range(16)]
    upper_all = jnp.zeros((16, 128), F32)
    inverse_all = jnp.zeros((16, 128), F32)
    for j in range(16):
        pivot = left[j][place[j]:place[j] + 1, :]
        root = lax.rsqrt(pivot)
        root = root * (1.5 - 0.5 * pivot * root * root)
        upper_row = left[j] * root
        inverse_row = right[j] * root
        for i in range(j + 1, 16):
            scale = upper_row[place[i]:place[i] + 1, :]
            left[i] = left[i] - scale * upper_row
            right[i] = right[i] - scale * inverse_row
        upper_row = jnp.where(natural >= j, upper_row, 0.0)
        if j:
            upper_row = pltpu.roll(upper_row, j, 1)
            inverse_row = pltpu.roll(inverse_row, j, 1)
        upper_all = jnp.where(lane == j, upper_row, upper_all)
        inverse_all = jnp.where(lane == j, inverse_row, inverse_all)

    upper[...] = jnp.zeros_like(upper)
    upper[pl.ds(0, 8, stride=2), :] = upper_all[0:8]
    upper[pl.ds(1, 8, stride=2), :] = upper_all[8:16]
    factors[...] = jnp.transpose(upper[...])[:, 0:16].reshape(8, 16, 16)
    factors_copy = pltpu.make_async_copy(factors, factors_hbm, sems.at[0])
    factors_copy.start()

    inverse_all = inverse_all * math.sqrt(points)
    row_freq = lax.broadcasted_iota(jnp.int32, (128, 128), 0) // 16
    lane_freq = lax.broadcasted_iota(jnp.int32, (128, 128), 1) // 16
    wide = jnp.where(row_freq == lane_freq, jnp.concatenate([inverse_all] * 8, axis=0), 0.0)
    w_high, w_middle, w_low = split3(jnp.transpose(wide))
    product = lax.dot_general(
        jnp.concatenate([w_high, w_high, w_middle, w_middle, w_high, w_low], axis=1),
        jnp.concatenate([high, middle, high, middle, low, high], axis=0),
        (((1,), (0,)), ((), ())),
        preferred_element_type=F32,
    )
    modes[...] = product.reshape(8, 16, 256)
    modes_copy = pltpu.make_async_copy(modes, modes_hbm, sems.at[1])
    modes_copy.start()
    factors_copy.wait()
    modes_copy.wait()


def fused(snapshots):
    points = snapshots.shape[1]
    dma = pltpu.SemaphoreType.DMA
    vmem = pltpu.VMEM
    columns, gram = pl.pallas_call(
        functools.partial(kernel, points),
        out_shape=(
            jax.ShapeDtypeStruct((128, 256), F32),
            jax.ShapeDtypeStruct((16, 128), F32),
        ),
        in_specs=[pl.BlockSpec(memory_space=pltpu.HBM)],
        out_specs=(pl.BlockSpec(memory_space=pltpu.VMEM),) * 2,
        scratch_shapes=[
            vmem((8, 64, 1024), F32),
            vmem((48, 192), BF16),
            vmem((8, 2, 2, 16, 256), F32),
            vmem((8, 2, 16, 256), F32),
            vmem((8, 16, 256), F32),
            vmem((8, 16, 256), F32),
            vmem((8, 2, 16, 128), F32),
            vmem((2, 128, 128), F32),
            vmem((16, 128), F32),
            vmem((8, 16, 128), F32),
            vmem((16, 128), F32),
            vmem((4, 16, 128), F32),
            dma((8,)),
            dma((8,)),
            dma((8,)),
            dma((8,)),
            dma((8,)),
            dma((8,)),
            dma((8,)),
            dma((8,)),
            dma((8,)),
            dma((4,)),
            dma((4,)),
        ],
        compiler_params=pltpu.CompilerParams(
            collective_id=0, has_side_effects=True, vmem_limit_bytes=53 * 1024 * 1024
        ),
        name="welch_gram",
    )(snapshots)
    return pl.pallas_call(
        functools.partial(finish_kernel, points),
        out_shape=(
            jax.ShapeDtypeStruct((8, 16, 16), F32),
            jax.ShapeDtypeStruct((8, 16, 256), F32),
        ),
        in_specs=[pl.BlockSpec(memory_space=pltpu.VMEM)] * 2,
        out_specs=(pl.BlockSpec(memory_space=pl.ANY),) * 2,
        scratch_shapes=[
            vmem((128, 128), F32),
            vmem((8, 16, 16), F32),
            vmem((8, 16, 256), F32),
            dma((2,)),
        ],
        compiler_params=pltpu.CompilerParams(vmem_limit_bytes=16 * 1024 * 1024),
        name="factor_modes",
    )(gram, columns)


def local(snapshots):
    time_dev, points = snapshots.shape
    n_aa = lax.axis_size("aa")
    n_ba = lax.axis_size("ba")
    if (n_aa, n_ba, time_dev, points) == (8, 4, 64, 8192):
        return fused(snapshots)
    pts_dev = points // (n_aa * n_ba)
    block_len = time_dev * n_ba
    table = spectral_table(block_len, points)
    regrouped = lax.all_to_all(
        lax.all_to_all(snapshots, "aa", split_axis=1, concat_axis=0, tiled=True),
        "ba",
        split_axis=1,
        concat_axis=0,
        tiled=True,
    )
    arranged = regrouped.reshape(n_ba, n_aa, time_dev, pts_dev)
    table_parts = table.reshape(n_ba, time_dev, 2, FREQS)
    spectra = jnp.einsum("uasp,usgf->agfp", arranged, table_parts, precision=lax.Precision.HIGHEST)
    blocks = spectra.shape[0]
    columns = 2 * blocks
    product = jnp.einsum("bgfp,chfp->fbgch", spectra, spectra, precision=lax.Precision.HIGHEST)
    gram_sum = lax.psum(product.reshape(FREQS, columns, columns), ("aa", "ba"))
    lower_factor = jnp.linalg.cholesky(gram_sum)
    identity = jnp.broadcast_to(jnp.eye(columns, dtype=gram_sum.dtype), lower_factor.shape)
    inverse = lax.linalg.triangular_solve(lower_factor, identity, left_side=True, lower=True)
    pod_modes = math.sqrt(points) * jnp.einsum(
        "fibg,bgfp->fip",
        inverse.reshape(FREQS, columns, blocks, 2),
        spectra,
        precision=lax.Precision.HIGHEST,
    )
    return (jnp.swapaxes(lower_factor, 1, 2), pod_modes)


def solution(mesh):
    placed = (P(("aa", "ba"), None),)
    return jax.shard_map(
        local,
        mesh=mesh,
        in_specs=placed,
        out_specs=(P(), P(None, None, ("aa", "ba"))),
        check_vma=False,
    )
```
